512 devices in a mesh: dp: 32 (over z, x), proto: 16 (over y, core).
Axes of the slice: x: 4, y: 8, z: 8, core: 2. Of those that a mesh axis runs over, the one named last changes fastest.
Arguments:
- teacher: bfloat16 [4096, 384], P('dp'), may hold values from -6 to 6
- student: bfloat16 [4096, 384], P('dp'), may hold values from -6 to 6
- proto_weight: bfloat16 [384, 131072], P('dp', 'proto'), may hold values from -0.6 to 0.6
- cotangent: float32 [4096], P('dp'), may hold values from 64 to 1024
Outputs:
- crop_loss: float32 [4096], P('dp')
- feature_grad: float32 [4096, 384], P('dp')
The draws below stay inside these ranges and needn't reach their ends.
All inputs are finite; a program needn't handle non-finite values.
Results may differ from the reference program's by a relative error of at most 0.0028.
Values may be sent and summed in bfloat16 or wider, within the bound.
A program may use at most 64 MiB of HBM per device.

```python
import math
import jax
import jax.numpy as jnp
from jax import lax

D = 384
K = 131072
B_DEV = 128
ITERS = 3
TOKENS = 4096


def draw_teacher(key, part):
    key = jax.random.fold_in(key, 11)
    mean_key, jitter_key, rest_key = jax.random.split(key, 3)
    shard_count = TOKENS // B_DEV
    shard_means = jax.random.normal(mean_key, (shard_count, 8), jnp.float32)
    jitter = jax.random.normal(jitter_key, (TOKENS, 8), jnp.float32)
    own_means = jnp.repeat(shard_means, B_DEV, axis=0)
    leading = jnp.clip(1.5 * (own_means + jitter), -6.0, 6.0)
    remainder = jnp.clip(0.2 * jax.random.normal(rest_key, (TOKENS, D - 8), jnp.float32), -6.0, 6.0)
    return jnp.concatenate([leading, remainder], axis=1).astype(jnp.bfloat16)


def draw_proto_weight(key, part):
    key = jax.random.fold_in(key, 23)
    mean_key, jitter_key, rest_key = jax.random.split(key, 3)
    block_means = jax.random.normal(mean_key, (16, 8), jnp.float32)
    jitter = jax.random.normal(jitter_key, (K, 8), jnp.float32)
    block_index = jnp.arange(K, dtype=jnp.int32) * 16 // K
    column_means = block_means[block_index]
    leading = jnp.clip(column_means + jitter, -5.97, 5.97).T
    remainder = jnp.clip(0.15 * jax.random.normal(rest_key, (D - 8, K), jnp.float32), -5.97, 5.97)
    return (0.1 * jnp.concatenate([leading, remainder], axis=0)).astype(jnp.bfloat16)


def shard_levels(own_key, shape, shards, least, high):
    def one(axis_at, blocks):
        draws = jax.random.uniform(jax.random.fold_in(jax.random.fold_in(own_key, 6), axis_at), (blocks,), jnp.float32, least / len(shards), high / len(shards))
        return jnp.repeat(jnp.exp(draws), shape[axis_at] // blocks).reshape((-1,) + (1,) * (len(shape) - axis_at - 1))

    level = one(*shards[0])
    for cut in shards[1:]:
        level = level * one(*cut)
    return level


def noise(key, dims, spread, bound, cuts=(), kind=jnp.bfloat16):
    drawn = jax.random.normal(key, dims, jnp.float32) * spread
    if len(cuts) > 0:
        drawn = shard_levels(key, dims, cuts, -0.22, 0.18) * drawn
    return jnp.clip(drawn, min=-bound, max=bound).astype(kind)


def setup_inputs(seed: int = 0) -> dict:
    splits = jax.random.split(jax.random.key(seed), 5)
    teacher = draw_teacher(jax.random.fold_in(splits[4], 71), 0)
    student = noise(splits[1], (TOKENS, D), 1.0, 6.0, ((0, 32),))
    proto_weight = draw_proto_weight(jax.random.fold_in(splits[4], 71), 0)
    cotangent = jnp.clip(jnp.exp(math.log(1024.0) - 2.7725887 * jax.random.uniform(splits[3], (TOKENS,), jnp.float32) ** shard_levels(splits[3], (TOKENS,), ((0, 32),), -0.2, 0.2)), 64.0, 1024.0)
    return {"teacher": teacher, "student": student, "proto_weight": proto_weight, "cotangent": cotangent}


epsilon = 1e-06
teacher_temp = 0.04
student_temp = 0.1

def normalize_rows(values):
    values_f = values.astype(jnp.float32)
    inv_norm = lax.rsqrt(lax.optimization_barrier(jnp.sum(values_f * values_f, axis=1, keepdims=True)) + epsilon)
    return (values_f * inv_norm, inv_norm)

def column_scale(shard_rows):
    weight_f = shard_rows.astype(jnp.float32)
    return lax.rsqrt(lax.optimization_barrier(jnp.sum(weight_f * weight_f, axis=0, keepdims=True)) + epsilon)

def reference(teacher, student, proto_weight, cotangent):
    teacher_norm, unused_inv = normalize_rows(teacher)
    teacher_unit = teacher_norm.astype(jnp.bfloat16)
    student_norm, inv_student = normalize_rows(student)
    student_unit = student_norm.astype(jnp.bfloat16)
    block_width = min(K, 8192)
    block_count = K // block_width
    blocks = proto_weight.reshape(D, block_count, block_width).transpose(1, 0, 2)

    def teacher_block(shard_rows):
        scores = jnp.dot(teacher_unit, shard_rows, preferred_element_type=jnp.float32)
        return jnp.exp(scores * column_scale(shard_rows) / teacher_temp)
    teacher_exp = lax.map(teacher_block, blocks)
    row_scale = jnp.ones((TOKENS,), jnp.float32)
    col_scale = jnp.ones((block_count, block_width), jnp.float32)
    for sweep in range(ITERS):
        col_scale = 1.0 / jnp.einsum('cbw,b->cw', teacher_exp, row_scale, precision=lax.Precision.HIGHEST)
        row_scale = 1.0 / jnp.einsum('cbw,cw->b', teacher_exp, col_scale, precision=lax.Precision.HIGHEST)
    row_column = row_scale[:, None]

    def student_logit_of(shard_rows):
        scores = jnp.dot(student_unit, shard_rows, preferred_element_type=jnp.float32)
        return scores * column_scale(shard_rows) / student_temp

    def student_step(running, current):
        exp_total, cross_term = running
        shard_rows, exp_block, scale_block = current
        logits = student_logit_of(shard_rows)
        target = exp_block * row_column * scale_block[None, :]
        return ((exp_total + lax.optimization_barrier(jnp.sum(jnp.exp(logits), axis=1)), cross_term + lax.optimization_barrier(jnp.sum(target * logits, axis=1))), None)
    zeros_rows = jnp.zeros((TOKENS,), jnp.float32)
    (exp_total, cross_term), unused = lax.scan(student_step, (zeros_rows, zeros_rows), (blocks, teacher_exp, col_scale))
    crop_loss = jnp.log(exp_total) - cross_term

    def grad_step(running, current):
        shard_rows, exp_block, scale_block = current
        logits = student_logit_of(shard_rows)
        target = exp_block * row_column * scale_block[None, :]
        soft = jnp.exp(logits) / exp_total[:, None]
        dscaled = (cotangent[:, None] * (soft - target) / student_temp * column_scale(shard_rows)).astype(jnp.bfloat16)
        term = lax.dot_general(dscaled, shard_rows, (((1,), (1,)), ((), ())), preferred_element_type=jnp.float32)
        return (running + term, None)
    unit_grad, unused = lax.scan(grad_step, jnp.zeros((TOKENS, D), jnp.float32), (blocks, teacher_exp, col_scale))
    along = lax.optimization_barrier(jnp.sum(student_norm * unit_grad, axis=1, keepdims=True))
    feature_grad = (unit_grad - student_norm * along) * inv_student
    return (crop_loss, feature_grad)
```

```python
import math

import jax
import jax.numpy as jnp
from jax import lax
from jax.experimental import pallas as pl
from jax.experimental.pallas import tpu as pltpu
from jax.sharding import PartitionSpec as P

EPS = 1e-06
LOG2E = math.log2(math.e)
T_SCALE = LOG2E / 0.04
S_SCALE = LOG2E / 0.1
F32, BF16 = jnp.float32, jnp.bfloat16
MESH = pl.DeviceIdType.MESH
HIGHEST = lax.Precision.HIGHEST
NT = (((1,), (1,)), ((), ()))

FAR_FIRST = (4, 3, 5, 2, 6, 1, 7)

T_Z, W_Z, S_Z = 0, 1, 3
RING = 4
COLS = 20
ROW_Y, ROW_Z = 23, 26
G1_A, G1_B, G2_A, G2_B, U_A, U_B, FIN, FIN_CORE = range(29, 37)
T_Y, S_Y = 37, 41
COUNT = 45


def unit_rows(values):
    inv = lax.rsqrt(jnp.sum(values * values, axis=1, keepdims=True) + EPS)
    return values * inv, inv


def fold(terms):
    while len(terms) > 1:
        terms = [a + b for a, b in zip(terms[::2], terms[1::2])]
    return terms[0]


def kernel(
    t_hbm, s_hbm, w_hbm, cot_hbm,
    grad_ref, loss_ref,
    t_ref, s_ref, w_ref, cot_ref, perm_ref,
    pack, wz_send, wz_buf, wz_wide, asm, wb,
    fz_send, fz_buf, ft, sz_send, sz_buf, fs,
    e_ref, l_ref, pb, rowacc, rowacc2, eacc, rb, xb, ivec, cvec,
    c_send, c_buf, ry_send, ry_buf, rz_send, rz_buf,
    ga, gb, g1a_send, g1a_buf, g1b_send, g1b_buf, g2a_send, g2a_buf, g2b_send, g2b_buf,
    ua_send, ua_buf, ub_send, ub_buf, csum, vec, lry_send, lry_buf, lrz_send, lrz_buf,
    col_cot, col_x, own_unit,
    fin_send, fin_buf,
    lsem, ssem, rsem,
):
    dp, pr = lax.axis_index("dp"), lax.axis_index("proto")
    z, x = lax.div(dp, 4), lax.rem(dp, 4)
    y, k = lax.div(pr, 2), lax.rem(pr, 2)

    def z_peer(i):
        return (lax.rem(z + i, 8) * 4 + x, pr)

    def y_peer(i):
        return (dp, lax.rem(y + i, 8) * 2 + k)

    def xk_peer(i):
        g = lax.rem(x * 2 + k + i, 8)
        return (z * 4 + lax.div(g, 2), y * 2 + lax.rem(g, 2))

    def a_peer(i):
        y_at, z_at = y_peer(i)[1], z_peer(i)[0]
        return (dp + k * (z_at - dp), y_at + k * (pr - y_at))

    def b_peer(i):
        y_at, z_at = y_peer(i)[1], z_peer(i)[0]
        return (z_at + k * (dp - z_at), pr + k * (y_at - pr))

    a_me, b_me = y + k * (z - y), z + k * (y - z)
    a_step, b_step = 64 - 56 * k, 8 + 56 * k

    def crops(a, b):
        return pl.ds(pl.multiple_of(a * a_step + b * b_step, 8), 8)

    def copy(src, dst, sem, peer):
        return pltpu.make_async_remote_copy(
            src_ref=src, dst_ref=dst, send_sem=ssem.at[sem], recv_sem=rsem.at[sem],
            device_id=peer, device_id_type=MESH,
        )

    def got(ref, sem):
        copy(ref, ref, sem, (dp, pr)).wait_recv()

    def sent(ref, sem):
        copy(ref, ref, sem, (dp, pr)).wait_send()

    half = lax.rem(y, 2)
    at16 = pl.multiple_of(k * 64 + lax.div(y, 2) * 16, 16)
    rows16 = pl.ds(at16, 16)
    loads = [
        pltpu.make_async_copy(src, dst, lsem.at[n])
        for n, (src, dst) in enumerate((
            (t_hbm.at[rows16], t_ref), (w_hbm, w_ref), (s_hbm.at[rows16], s_ref), (cot_hbm, cot_ref)
        ))
    ]
    for load in loads:
        load.start()

    barrier = pltpu.get_barrier_semaphore()
    for i in range(1, 8):
        for peer in (z_peer(i), y_peer(i), xk_peer(i)):
            pl.semaphore_signal(barrier, inc=1, device_id=peer, device_id_type=MESH)

    feature = lax.broadcasted_iota(jnp.int32, (384, 128), 0)
    fz = lax.shift_right_logical(feature * 1366, 16)
    fx = lax.shift_right_logical((feature - fz * 48) * 5462, 16)
    place = fx * 96 + fz * 12 + (feature - fz * 48 - fx * 12)
    lane = lax.broadcasted_iota(jnp.int32, (384, 128), 1)
    for n in range(3):
        perm_ref[:, 128 * n:128 * n + 128] = (place == lane + 128 * n).astype(F32).astype(BF16)

    def own_rows(ref, send, buf):
        v = unit_rows(ref[...].astype(F32))[0].astype(BF16)
        v = jnp.dot(v, perm_ref[...], preferred_element_type=F32)
        v = jnp.where(half == 0, v[0:8], v[8:16])
        send[...] = v
        buf[z] = v

    loads[0].wait()
    own_rows(t_ref, fz_send, fz_buf)
    loads[1].wait()
    for d in range(8):
        for h in range(2):
            for r in range(4):
                q, at = d * 8 + h * 4 + r, ((h * 8 + d) * 4 + r) * 12
                pack[at:at + 12, :] = w_ref[:, 128 * q:128 * q + 128].astype(F32)
    for h in range(2):
        for d in range(8):
            at = (h * 8 + d) * 48
            wz_send[h, d] = pack[at:at + 48, :].astype(BF16)
        wz_buf[h, z] = wz_send[h, z]

    pl.semaphore_wait(barrier, 21)

    for i in FAR_FIRST:
        copy(fz_send, fz_buf.at[z], T_Z, z_peer(i)).start()
    for h in range(2):
        for i in FAR_FIRST:
            copy(wz_send.at[h, lax.rem(z + i, 8)], wz_buf.at[h, z], W_Z + h, z_peer(i)).start()

    loads[2].wait()
    own_rows(s_ref, sz_send, sz_buf)
    for i in FAR_FIRST:
        copy(sz_send, sz_buf.at[z], S_Z, z_peer(i)).start()

    first, second = pl.ds(0, 32), pl.ds(32, 32)

    def rows_out(buf, at):
        block = buf.at[y]
        copy(block, block, at + 1, y_peer(2)).start()
        copy(block, block, at + 2, y_peer(6)).start()
        copy(block, block, at, y_peer(1)).start()
        copy(block, block, at, y_peer(7)).start()

    def rows_on(buf, at):
        below, above = buf.at[lax.rem(y + 6, 8)], buf.at[lax.rem(y + 2, 8)]
        got(below, at + 1)
        copy(below.at[first], below.at[first], at + 3, y_peer(2)).start()
        copy(below, below, at + 3, y_peer(1)).start()
        got(above, at + 2)
        copy(above.at[second], above.at[second], at + 3, y_peer(6)).start()
        copy(above, above, at + 3, y_peer(7)).start()

    def rows_in(buf, at):
        got(buf.at[pl.ds(0, 2)], at)
        got(buf.at[pl.ds(0, 3)], at + 3)

    got(fz_buf.at[pl.ds(0, 7)], T_Z)
    ft[y] = fz_buf[...].reshape(64, 384).astype(BF16)
    rows_out(ft, T_Y)

    x_right, x_left, x_far = lax.rem(x + 1, 4), lax.rem(x + 3, 4), lax.rem(x + 2, 4)
    right, left, core = (z * 4 + x_right, pr), (z * 4 + x_left, pr), (dp, y * 2 + 1 - k)
    low, high = pl.ds(0, 48), pl.ds(48, 48)

    def piece(h, at):
        return wb.at[h, k, at]

    for h in range(2):
        got(wz_buf.at[h, pl.ds(0, 7)], W_Z + h)
        for s in range(8):
            wz_wide[s] = wz_buf[h, s].astype(F32)
            for q in range(4):
                asm[12 * s:12 * s + 12, 128 * q:128 * q + 128] = wz_wide[s, 12 * q:12 * q + 12, :]
        wb[h, k, x] = asm[...].astype(BF16)
        own = piece(h, x)
        copy(own, own, RING + 8 * h, right).start()
        copy(own, own, RING + 8 * h + 1, left).start()
        copy(own, own, RING + 8 * h + 4, core).start()
        if h == 0:
            rows_on(ft, T_Y)
    got(sz_buf.at[pl.ds(0, 7)], S_Z)
    fs[y] = sz_buf[...].reshape(64, 384).astype(BF16)
    rows_out(fs, S_Y)
    for h in range(2):
        at, from_left, from_right = RING + 8 * h, piece(h, x_left), piece(h, x_right)
        got(from_left, at)
        copy(from_left.at[low], from_left.at[low], at + 2, right).start()
        got(from_right, at + 1)
        copy(from_right.at[high], from_right.at[high], at + 3, left).start()
        copy(from_left, from_left, at + 5, core).start()
        copy(from_right, from_right, at + 6, core).start()

    def far_piece(h):
        far = piece(h, x_far)
        got(far.at[low], RING + 8 * h + 2)
        got(far.at[high], RING + 8 * h + 3)
        copy(far, far, RING + 8 * h + 7, core).start()

    far_piece(0)
    rows_in(ft, T_Y)
    far_piece(1)

    def chunk(q):
        h, kk, c0 = lax.div(q, 4), lax.rem(lax.div(q, 2), 2), pl.multiple_of(lax.rem(q, 2) * 256, 256)
        return wb[h, kk, :, :, pl.ds(c0, 256)].reshape(384, 256), pl.ds(pl.multiple_of(q * 256, 256), 256)

    def teacher_chunk(q, carry):
        w, at = chunk(q)
        wf = w.astype(F32)
        inv = lax.rsqrt(jnp.sum(wf * wf, axis=0, keepdims=True) + EPS)
        scores = jnp.dot(ft[...].reshape(512, 384), w, preferred_element_type=F32)
        e = jnp.exp2(scores * (inv * T_SCALE))
        e_ref[:, at] = e
        col = jnp.sum(e, axis=0, keepdims=True)
        for n in range(2):
            part = slice(128 * n, 128 * n + 128)
            ivec[pl.ds(2 * q + n, 1), :] = inv[:, part]
            csum[pl.ds(2 * q + n, 1), :] = col[:, part]
        return carry

    for h in range(2):
        for n in range(4):
            got(piece(h, x), RING + 8 * h + 4 + n)
        lax.fori_loop(4 * h, 4 * h + 4, teacher_chunk, 0)
        if h == 0:
            rows_on(fs, S_Y)

    def columns_start(it):
        c_send[it] = csum[...].astype(BF16)
        for i in FAR_FIRST:
            copy(c_send.at[it], c_buf.at[it, i - 1], COLS + it, xk_peer(i)).start()

    def columns_end(it):
        got(c_buf.at[it], COLS + it)
        cvec[...] = 1.0 / fold([c_send[it].astype(F32)] + [c_buf[it, i].astype(F32) for i in range(7)])

    def row_pass():
        scale = [cvec[q:q + 1, :] for q in range(16)]

        def body(i, carry):
            rows = pl.ds(pl.multiple_of(i * 16, 16), 16)
            rowacc[rows, :] = fold([e_ref[rows, 128 * q:128 * q + 128] * scale[q] for q in range(16)])
            return carry

        lax.fori_loop(0, 32, body, 0, unroll=4)

    def lanes(ref):
        return [jnp.sum(jnp.transpose(ref[128 * j:128 * j + 128, :]), axis=0, keepdims=True) for j in range(4)]

    def put(dst, at, sums):
        for j in range(4):
            dst[at + j:at + j + 1, :] = sums[j]

    def row_refs(it):
        if it == 2:
            return lry_send, lry_buf, lrz_send, lrz_buf
        return ry_send.at[it], ry_buf.at[it], rz_send.at[it], rz_buf.at[it]

    def added(own, buf):
        return fold([own[...]] + [buf[i] for i in range(7)])

    def rows_start(it):
        y_send, y_buf, _, _ = row_refs(it)
        put(y_send, 0, lanes(rowacc))
        for i in FAR_FIRST:
            copy(y_send, y_buf.at[i - 1], ROW_Y + it, y_peer(i)).start()

    def rows_middle(it):
        y_send, y_buf, z_send, z_buf = row_refs(it)
        got(y_buf, ROW_Y + it)
        z_send[...] = added(y_send, y_buf)
        for i in FAR_FIRST:
            copy(z_send, z_buf.at[i - 1], ROW_Z + it, z_peer(i)).start()

    def turn(row):
        return jnp.transpose(jnp.broadcast_to(row, (128, 128)))

    def rows_end(it):
        _, _, z_send, z_buf = row_refs(it)
        got(z_buf, ROW_Z + it)
        total = added(z_send, z_buf)
        r = 1.0 / total[0:4, :]
        for j in range(4):
            rb[128 * j:128 * j + 128, :] = turn(r[j:j + 1, :])
        return total

    def column_pass():
        def body(i, acc):
            rows = pl.ds(pl.multiple_of(i * 8, 8), 8)
            r8 = rb[rows, :]
            return tuple(acc[q] + e_ref[rows, 128 * q:128 * q + 128] * r8 for q in range(16))

        acc = lax.fori_loop(0, 64, body, tuple(jnp.zeros((8, 128), F32) for _ in range(16)), unroll=4)
        for q in range(16):
            csum[q:q + 1, :] = jnp.sum(acc[q], axis=0, keepdims=True)

    def student_chunk(q, carry):
        w, at = chunk(q)
        inv = jnp.concatenate([ivec[pl.ds(2 * q, 1), :], ivec[pl.ds(2 * q + 1, 1), :]], axis=1)
        logits = jnp.dot(fs[...].reshape(512, 384), w, preferred_element_type=F32) * (inv * S_SCALE)
        l_ref[:, at] = logits
        p = jnp.exp2(logits)
        eacc[...] += p[:, :128] + p[:, 128:]
        pb[:, at] = (p * inv).astype(BF16)
        return carry

    def product(first, last):
        total = None
        for n in range(4):
            h, kk = divmod(n, 2)
            term = lax.dot_general(
                pb[:, 512 * n:512 * n + 512], wb[h, kk].reshape(384, 512)[first:last], NT, preferred_element_type=F32
            )
            total = term if total is None else total + term
        return total

    def gradient_a(dst):
        ga[...] = product(0, 256)
        for a in range(8):
            dst[a] = jnp.concatenate([ga[crops(a, b), :] for b in range(8)], axis=0).astype(BF16)

    def gradient_b(dst):
        gb[...] = product(256, 384)
        for b in range(8):
            dst[b] = jnp.concatenate([gb[crops(a, b), :] for a in range(8)], axis=0).astype(BF16)

    def spread_a(src, dst, sem):
        for i in FAR_FIRST:
            copy(src.at[lax.rem(a_me + i, 8)], dst.at[i - 1], sem, a_peer(i)).start()

    def spread_b(src, dst, sem):
        for i in FAR_FIRST:
            copy(src.at[lax.rem(b_me + i, 8)], dst.at[i - 1], sem, b_peer(i)).start()

    columns_start(0)
    lry_send[...] = jnp.zeros_like(lry_send)
    eacc[...] = jnp.zeros_like(eacc)
    loads[3].wait()
    col_cot[...] = turn(cot_ref[...])
    columns_end(0)
    row_pass()
    rows_start(0)
    rows_in(fs, S_Y)
    lax.fori_loop(0, 2, student_chunk, 0)
    rows_middle(0)
    lax.fori_loop(2, 5, student_chunk, 0)
    rows_end(0)
    column_pass()
    columns_start(1)
    lax.fori_loop(5, 8, student_chunk, 0)
    columns_end(1)
    row_pass()
    rows_start(1)
    gradient_a(g1a_send)
    rows_middle(1)
    spread_a(g1a_send, g1a_buf, G1_A)
    gradient_b(g1b_send)
    rows_end(1)
    spread_b(g1b_send, g1b_buf, G1_B)
    column_pass()
    columns_start(2)
    s16 = unit_rows(s_ref[...].astype(F32))
    s8, inv8 = (jnp.where(half == 0, v[0:8], v[8:16]) for v in s16)
    put(lry_send, 8, lanes(eacc))
    own_unit[...] = jnp.dot(s8, perm_ref[...].astype(F32), precision=HIGHEST, preferred_element_type=F32)
    columns_end(2)

    c_rows = [cvec[q:q + 1, :] for q in range(16)]
    i_rows = [ivec[q:q + 1, :] for q in range(16)]

    def last_pass(i, carry):
        rows = pl.ds(pl.multiple_of(i * 16, 16), 16)
        acc, acc2 = [], []
        for q in range(16):
            at = slice(128 * q, 128 * q + 128)
            v = e_ref[rows, at] * c_rows[q]
            acc.append(v)
            acc2.append(v * l_ref[rows, at])
            pb[rows, at] = (v * i_rows[q]).astype(BF16)
        rowacc[rows, :] = fold(acc)
        rowacc2[rows, :] = fold(acc2)
        return carry

    lax.fori_loop(0, 32, last_pass, 0, unroll=2)
    put(lry_send, 4, lanes(rowacc2))
    rows_start(2)
    gradient_a(g2a_send)
    spread_a(g2a_send, g2a_buf, G2_A)
    gradient_b(g2b_send)
    rows_middle(2)
    spread_b(g2b_send, g2b_buf, G2_B)

    def sum_blocks(own, buf):
        return fold([own.astype(F32)] + [buf[i].astype(F32) for i in range(7)])

    def wide(block, times):
        return jnp.concatenate([block] * times, axis=1)

    got(g1a_buf, G1_A)
    got(g1b_buf, G1_B)
    g1a = sum_blocks(g1a_send[a_me], g1a_buf)
    g1b = sum_blocks(g1b_send[b_me], g1b_buf)
    total = rows_end(2)
    vec[...] = total
    inv_total = 1.0 / total[8:12, :]
    for j in range(4):
        xb[128 * j:128 * j + 128, :] = turn(inv_total[j:j + 1, :])
    col_x[...] = turn(vec[pl.ds(lax.div(y, 2) + 4, 1), :])
    got(g2b_buf, G2_B)
    g2b = sum_blocks(g2b_send[b_me], g2b_buf)
    for a in range(8):
        rows, part = crops(a, b_me), slice(8 * a, 8 * a + 8)
        ub_send[a] = g1b[part] * xb[rows, :] - g2b[part] * rb[rows, :]
    for i in FAR_FIRST:
        copy(ub_send.at[lax.rem(a_me + i, 8)], ub_buf.at[i - 1], U_B, a_peer(i)).start()
    got(g2a_buf, G2_A)
    g2a = sum_blocks(g2a_send[a_me], g2a_buf)
    for b in range(8):
        rows, part = crops(a_me, b), slice(8 * b, 8 * b + 8)
        ua_send[b] = g1a[part] * wide(xb[rows, :], 2) - g2a[part] * wide(rb[rows, :], 2)
    for i in FAR_FIRST:
        copy(ua_send.at[lax.rem(b_me + i, 8)], ua_buf.at[i - 1], U_A, b_peer(i)).start()

    rows8 = pl.ds(pl.multiple_of(y * 64 + z * 8, 8), 8)
    cross = rb[rows8, :] * col_x[pl.ds(pl.multiple_of(half * 64 + z * 8, 8), 8), :]
    loss8 = -jnp.log(xb[rows8, :]) - math.log(2.0) * cross
    cot8 = wide(col_cot[pl.ds(pl.multiple_of(k * 64 + y * 8, 8), 8), :], 3)
    got(ub_buf, U_B)
    u_b = added(ub_send.at[a_me], ub_buf)
    got(ua_buf, U_A)
    u8 = jnp.concatenate([added(ua_send.at[b_me], ua_buf), u_b], axis=1) * (cot8 / 0.1)
    unit8 = own_unit[...]
    along = jnp.sum(unit8 * u8, axis=1, keepdims=True)
    result = ((u8 - unit8 * along) * inv8).astype(BF16)
    result = lax.dot_general(result, perm_ref[...], NT, preferred_element_type=F32)
    first = loss8.astype(BF16).astype(F32)
    loss8 = jnp.where(lax.broadcasted_iota(jnp.int32, (8, 128), 1) < 64, first, loss8 - first)
    low_rows, high_rows = result[:, :256], jnp.concatenate([result[:, 256:], loss8], axis=1)
    result = jnp.concatenate([low_rows, high_rows], axis=0).astype(BF16)
    fin_send[...] = result
    fin_buf[k, y] = result
    for i in FAR_FIRST:
        copy(fin_send, fin_buf.at[k, y], FIN, y_peer(i)).start()
    got(fin_buf.at[k, pl.ds(0, 7)], FIN)
    copy(fin_buf.at[k], fin_buf.at[k], FIN_CORE, core).start()
    got(fin_buf.at[1 - k], FIN_CORE)
    out = fin_buf[...].reshape(16, 16, 256).astype(F32)
    grad_ref[:, :256] = out[:, :8, :].reshape(128, 256)
    grad_ref[:, 256:] = out[:, 8:, :128].reshape(128, 128)
    losses = jnp.transpose(out[:, 8:, 128:].reshape(128, 128))
    loss_ref[...] = losses[0:1, :] + losses[64:65, :]

    sent(fz_buf.at[pl.ds(0, 7)], T_Z)
    sent(sz_buf.at[pl.ds(0, 7)], S_Z)
    for buf, at in ((ft, T_Y), (fs, S_Y)):
        sent(buf.at[pl.ds(0, 2)], at)
        sent(buf.at[y], at + 1)
        sent(buf.at[y], at + 2)
        sent(buf.at[pl.ds(0, 3)], at + 3)
    for h in range(2):
        at, own = RING + 8 * h, piece(h, x)
        sent(wz_buf.at[h, pl.ds(0, 7)], W_Z + h)
        sent(own, at)
        sent(own, at + 1)
        sent(own.at[low], at + 2)
        sent(own.at[low], at + 3)
        for n in range(4):
            sent(own, at + 4 + n)
    for it in range(3):
        sent(c_buf.at[it], COLS + it)
        _, y_buf, _, z_buf = row_refs(it)
        sent(y_buf, ROW_Y + it)
        sent(z_buf, ROW_Z + it)
    for buf, sem in (
        (g1a_buf, G1_A), (g1b_buf, G1_B), (g2a_buf, G2_A), (g2b_buf, G2_B), (ua_buf, U_A), (ub_buf, U_B),
        (fin_buf.at[k, pl.ds(0, 7)], FIN), (fin_buf.at[k], FIN_CORE),
    ):
        sent(buf, sem)


def shards(teacher, student, proto_weight, cotangent):
    vmem, hbm = pl.BlockSpec(memory_space=pltpu.VMEM), pl.BlockSpec(memory_space=pltpu.HBM)
    v = pltpu.VMEM
    operands = (teacher, student, proto_weight, cotangent.reshape(1, 128))
    grad, loss = pl.pallas_call(
        kernel,
        out_shape=(v((128, 384), F32), v((1, 128), F32)),
        in_specs=[hbm] * 4,
        out_specs=(vmem, vmem),
        scratch_shapes=[
            v((16, 384), BF16), v((16, 384), BF16), v((12, 8192), BF16), v((1, 128), F32), v((384, 384), BF16),
            v((768, 128), F32), v((2, 8, 48, 128), BF16), v((2, 8, 48, 128), BF16), v((8, 48, 128), F32),
            v((96, 512), F32), v((2, 2, 4, 96, 512), BF16),
            v((8, 384), F32), v((8, 8, 384), F32), v((8, 64, 384), BF16),
            v((8, 384), F32), v((8, 8, 384), F32), v((8, 64, 384), BF16),
            v((512, 2048), F32), v((512, 2048), F32), v((512, 2048), BF16),
            v((512, 128), F32), v((512, 128), F32), v((512, 128), F32), v((512, 128), F32), v((512, 128), F32),
            v((16, 128), F32), v((16, 128), F32),
            v((3, 16, 128), BF16), v((3, 7, 16, 128), BF16),
            v((2, 4, 128), F32), v((2, 7, 4, 128), F32), v((2, 4, 128), F32), v((2, 7, 4, 128), F32),
            v((512, 256), F32), v((512, 128), F32),
            v((8, 64, 256), BF16), v((7, 64, 256), BF16), v((8, 64, 128), BF16), v((7, 64, 128), BF16),
            v((8, 64, 256), BF16), v((7, 64, 256), BF16), v((8, 64, 128), BF16), v((7, 64, 128), BF16),
            v((8, 8, 256), F32), v((7, 8, 256), F32), v((8, 8, 128), F32), v((7, 8, 128), F32),
            v((16, 128), F32), v((16, 128), F32), v((16, 128), F32), v((7, 16, 128), F32), v((16, 128), F32), v((7, 16, 128), F32),
            v((128, 128), F32), v((128, 128), F32), v((8, 384), F32),
            v((16, 256), BF16), v((2, 8, 16, 256), BF16),
            pltpu.SemaphoreType.DMA((4,)), pltpu.SemaphoreType.DMA((COUNT,)), pltpu.SemaphoreType.DMA((COUNT,)),
        ],
        compiler_params=pltpu.CompilerParams(
            collective_id=0, has_side_effects=True, vmem_limit_bytes=60 * 1024 * 1024
        ),
        cost_estimate=pl.CostEstimate(flops=2_400_000_000, bytes_accessed=4_000_000, transcendentals=2_000_000),
    )(*(pltpu.with_memory_space_constraint(a, pltpu.HBM) for a in operands))
    return loss.reshape(128), grad


def solution(mesh):
    return jax.shard_map(
        shards,
        mesh=mesh,
        in_specs=(P("dp", None), P("dp", None), P("dp", "proto"), P("dp")),
        out_specs=(P("dp"), P("dp", None)),
        check_vma=False,
    )
```

```python
import math

import jax
import jax.numpy as jnp
from jax import lax
from jax.experimental import pallas as pl
from jax.experimental.pallas import tpu as pltpu
from jax.sharding import PartitionSpec as P

EPS = 1e-06
LOG2E = math.log2(math.e)
T_SCALE = LOG2E / 0.04
S_SCALE = LOG2E / 0.1
F32, BF16 = jnp.float32, jnp.bfloat16
MESH = pl.DeviceIdType.MESH
HIGHEST = lax.Precision.HIGHEST
NT = (((1,), (1,)), ((), ()))

FAR_FIRST = (4, 3, 5, 2, 6, 1, 7)

F_Z, W_Z = 0, 1
RING = 4
COLS = 24
ROW_Y, ROW_Z = 27, 30
G1_A, G1_B, G2_A, G2_B, U_A, U_B, FIN, FIN_CORE = range(33, 41)
T_Y, S_Y = 41, 45
COUNT = 49


def unit_rows(values):
    inv = lax.rsqrt(jnp.sum(values * values, axis=1, keepdims=True) + EPS)
    return values * inv, inv


def fold(terms):
    while len(terms) > 1:
        terms = [a + b for a, b in zip(terms[::2], terms[1::2])]
    return terms[0]


def kernel(
    t_hbm, s_hbm, w_hbm, cot_hbm,
    grad_ref, loss_ref,
    t_ref, s_ref, w_ref, cot_ref, perm_ref,
    pack, wz_send, wz_buf, wz_wide, asm, wb,
    fz_send, fz_buf, ft, fs,
    e_ref, l_ref, pb, rowacc, rowacc2, eacc, rb, xb, ivec, cvec,
    c_send, c_buf, ry_send, ry_buf, rz_send, rz_buf,
    ga, gb, g1a_send, g1a_buf, g1b_send, g1b_buf, g2a_send, g2a_buf, g2b_send, g2b_buf,
    ua_send, ua_buf, ub_send, ub_buf, csum, vec, lry_send, lry_buf, lrz_send, lrz_buf,
    col_cot, col_x, own_unit,
    fin_send, fin_buf,
    lsem, ssem, rsem,
):
    dp, pr = lax.axis_index("dp"), lax.axis_index("proto")
    z, x = lax.div(dp, 4), lax.rem(dp, 4)
    y, k = lax.div(pr, 2), lax.rem(pr, 2)

    def z_peer(i):
        return (lax.rem(z + i, 8) * 4 + x, pr)

    def y_peer(i):
        return (dp, lax.rem(y + i, 8) * 2 + k)

    def xk_peer(i):
        g = lax.rem(x * 2 + k + i, 8)
        return (z * 4 + lax.div(g, 2), y * 2 + lax.rem(g, 2))

    def a_peer(i):
        y_at, z_at = y_peer(i)[1], z_peer(i)[0]
        return (dp + k * (z_at - dp), y_at + k * (pr - y_at))

    def b_peer(i):
        y_at, z_at = y_peer(i)[1], z_peer(i)[0]
        return (z_at + k * (dp - z_at), pr + k * (y_at - pr))

    a_me, b_me = y + k * (z - y), z + k * (y - z)
    a_step, b_step = 64 - 56 * k, 8 + 56 * k

    def crops(a, b):
        return pl.ds(pl.multiple_of(a * a_step + b * b_step, 8), 8)

    def copy(src, dst, sem, peer):
        return pltpu.make_async_remote_copy(
            src_ref=src, dst_ref=dst, send_sem=ssem.at[sem], recv_sem=rsem.at[sem],
            device_id=peer, device_id_type=MESH,
        )

    def got(ref, sem):
        copy(ref, ref, sem, (dp, pr)).wait_recv()

    def sent(ref, sem):
        copy(ref, ref, sem, (dp, pr)).wait_send()

    half = lax.rem(y, 2)
    at16 = pl.multiple_of(k * 64 + lax.div(y, 2) * 16, 16)
    rows16 = pl.ds(at16, 16)
    loads = [
        pltpu.make_async_copy(src, dst, lsem.at[n])
        for n, (src, dst) in enumerate((
            (t_hbm.at[rows16], t_ref), (w_hbm, w_ref), (s_hbm.at[rows16], s_ref), (cot_hbm, cot_ref)
        ))
    ]
    for load in loads:
        load.start()

    barrier = pltpu.get_barrier_semaphore()
    for i in range(1, 8):
        for peer in (z_peer(i), y_peer(i), xk_peer(i)):
            pl.semaphore_signal(barrier, inc=1, device_id=peer, device_id_type=MESH)

    feature = lax.broadcasted_iota(jnp.int32, (384, 128), 0)
    fz = lax.shift_right_logical(feature * 1366, 16)
    fx = lax.shift_right_logical((feature - fz * 48) * 5462, 16)
    place = fx * 96 + fz * 12 + (feature - fz * 48 - fx * 12)
    lane = lax.broadcasted_iota(jnp.int32, (384, 128), 1)
    for n in range(3):
        perm_ref[:, 128 * n:128 * n + 128] = (place == lane + 128 * n).astype(F32).astype(BF16)

    loads[0].wait()
    loads[2].wait()
    v = jnp.concatenate([t_ref[...].astype(F32), s_ref[...].astype(F32)], axis=0)
    v = jnp.dot(unit_rows(v)[0].astype(BF16), perm_ref[...], preferred_element_type=F32)
    v = [jnp.where(half == 0, v[at:at + 8], v[at + 8:at + 16]) for at in (0, 16)]
    v = jnp.concatenate([m[:, 128 * n:128 * n + 128] for m in v for n in range(3)], axis=0).astype(BF16)
    fz_send[...] = v
    fz_buf[z] = v
    loads[1].wait()
    for d in range(8):
        for h in range(2):
            for r in range(4):
                q, at = d * 8 + h * 4 + r, ((h * 8 + d) * 4 + r) * 12
                pack[at:at + 12, :] = w_ref[:, 128 * q:128 * q + 128].astype(F32)
    for h in range(2):
        for d in range(8):
            at = (h * 8 + d) * 48
            wz_send[h, d] = pack[at:at + 48, :].astype(BF16)
        wz_buf[h, z] = wz_send[h, z]

    pl.semaphore_wait(barrier, 21)

    for i in FAR_FIRST:
        copy(fz_send, fz_buf.at[z], F_Z, z_peer(i)).start()
    for h in range(2):
        for i in FAR_FIRST:
            copy(wz_send.at[h, lax.rem(z + i, 8)], wz_buf.at[h, z], W_Z + h, z_peer(i)).start()

    first, second = pl.ds(0, 32), pl.ds(32, 32)

    def rows_out(buf, at):
        block = buf.at[y]
        copy(block, block, at + 1, y_peer(2)).start()
        copy(block, block, at + 2, y_peer(6)).start()
        copy(block, block, at, y_peer(1)).start()
        copy(block, block, at, y_peer(7)).start()

    def rows_on(buf, at):
        below, above = buf.at[lax.rem(y + 6, 8)], buf.at[lax.rem(y + 2, 8)]
        got(below, at + 1)
        copy(below.at[first], below.at[first], at + 3, y_peer(2)).start()
        copy(below, below, at + 3, y_peer(1)).start()
        got(above, at + 2)
        copy(above.at[second], above.at[second], at + 3, y_peer(6)).start()
        copy(above, above, at + 3, y_peer(7)).start()

    def rows_in(buf, at):
        got(buf.at[pl.ds(0, 2)], at)
        got(buf.at[pl.ds(0, 3)], at + 3)

    got(fz_buf.at[pl.ds(0, 7)], F_Z)
    for buf, at in ((ft, 0), (fs, 24)):
        v = [fz_buf[d, :, :].astype(F32) for d in range(8)]
        v = [jnp.concatenate([m[at + 8 * n:at + 8 * n + 8] for m in v], axis=0) for n in range(3)]
        buf[y] = jnp.concatenate(v, axis=1).astype(BF16)
    rows_out(ft, T_Y)

    x_right, x_left, x_far = lax.rem(x + 1, 4), lax.rem(x + 3, 4), lax.rem(x + 2, 4)
    right, left, core = (z * 4 + x_right, pr), (z * 4 + x_left, pr), (dp, y * 2 + 1 - k)
    low, high = pl.ds(0, 48), pl.ds(48, 48)

    def piece(h, at):
        return wb.at[h, k, at]

    for h in range(2):
        got(wz_buf.at[h, pl.ds(0, 7)], W_Z + h)
        for s in range(8):
            wz_wide[s] = wz_buf[h, s].astype(F32)
            for q in range(4):
                asm[12 * s:12 * s + 12, 128 * q:128 * q + 128] = wz_wide[s, 12 * q:12 * q + 12, :]
        wb[h, k, x] = asm[...].astype(BF16)
        own = piece(h, x)
        at = RING + 10 * h
        copy(own.at[low], own.at[low], at, right).start()
        copy(own.at[high], own.at[high], at + 2, left).start()
        copy(own.at[high], own.at[high], at + 1, right).start()
        copy(own.at[low], own.at[low], at + 3, left).start()
        copy(own, own, at + 6, core).start()
        if h == 0:
            rows_on(ft, T_Y)
    rows_out(fs, S_Y)
    def relay(h):
        at, from_left, from_right = RING + 10 * h, piece(h, x_left), piece(h, x_right)
        got(from_left.at[low], at)
        copy(from_left.at[low], from_left.at[low], at + 4, right).start()
        got(from_right.at[high], at + 2)
        copy(from_right.at[high], from_right.at[high], at + 5, left).start()
        got(from_left.at[high], at + 1)
        copy(from_left, from_left, at + 7, core).start()
        got(from_right.at[low], at + 3)
        copy(from_right, from_right, at + 8, core).start()

    def far_piece(h):
        far = piece(h, x_far)
        got(far.at[low], RING + 10 * h + 4)
        got(far.at[high], RING + 10 * h + 5)
        copy(far, far, RING + 10 * h + 9, core).start()

    relay(0)
    far_piece(0)
    relay(1)
    rows_in(ft, T_Y)

    def chunk(q):
        h, kk, c0 = lax.div(q, 4), lax.rem(lax.div(q, 2), 2), pl.multiple_of(lax.rem(q, 2) * 256, 256)
        return wb[h, kk, :, :, pl.ds(c0, 256)].reshape(384, 256), pl.ds(pl.multiple_of(q * 256, 256), 256)

    def teacher_chunk(q, carry):
        w, at = chunk(q)
        wf = w.astype(F32)
        inv = lax.rsqrt(jnp.sum(wf * wf, axis=0, keepdims=True) + EPS)
        scores = jnp.dot(ft[...].reshape(512, 384), w, preferred_element_type=F32)
        e = jnp.exp2(scores * (inv * T_SCALE))
        e_ref[:, at] = e
        col = jnp.sum(e, axis=0, keepdims=True)
        for n in range(2):
            part = slice(128 * n, 128 * n + 128)
            ivec[pl.ds(2 * q + n, 1), :] = inv[:, part]
            csum[pl.ds(2 * q + n, 1), :] = col[:, part]
        return carry

    def teacher_part(h, kk):
        lax.fori_loop(0, 2, lambda c, carry: teacher_chunk(4 * h + 2 * kk + c, carry), 0)

    for h in range(2):
        if h == 1:
            far_piece(1)
        teacher_part(h, k)
        if h == 1:
            rows_on(fs, S_Y)
        for n in range(4):
            got(piece(h, x), RING + 10 * h + 6 + n)
        teacher_part(h, 1 - k)

    def columns_start(it):
        c_send[it] = csum[...].astype(BF16)
        for i in FAR_FIRST:
            copy(c_send.at[it], c_buf.at[it, i - 1], COLS + it, xk_peer(i)).start()

    def columns_end(it):
        got(c_buf.at[it], COLS + it)
        cvec[...] = 1.0 / fold([c_send[it].astype(F32)] + [c_buf[it, i].astype(F32) for i in range(7)])

    def row_pass():
        scale = [cvec[q:q + 1, :] for q in range(16)]

        def body(i, carry):
            rows = pl.ds(pl.multiple_of(i * 16, 16), 16)
            rowacc[rows, :] = fold([e_ref[rows, 128 * q:128 * q + 128] * scale[q] for q in range(16)])
            return carry

        lax.fori_loop(0, 32, body, 0, unroll=4)

    def lanes(ref):
        return [jnp.sum(jnp.transpose(ref[128 * j:128 * j + 128, :]), axis=0, keepdims=True) for j in range(4)]

    def put(dst, at, sums):
        for j in range(4):
            dst[at + j:at + j + 1, :] = sums[j]

    def row_refs(it):
        if it == 2:
            return lry_send, lry_buf, lrz_send, lrz_buf
        return ry_send.at[it], ry_buf.at[it], rz_send.at[it], rz_buf.at[it]

    def added(own, buf):
        return fold([own[...]] + [buf[i] for i in range(7)])

    def rows_start(it):
        y_send, y_buf, _, _ = row_refs(it)
        put(y_send, 0, lanes(rowacc))
        for i in FAR_FIRST:
            copy(y_send, y_buf.at[i - 1], ROW_Y + it, y_peer(i)).start()

    def rows_middle(it):
        y_send, y_buf, z_send, z_buf = row_refs(it)
        got(y_buf, ROW_Y + it)
        z_send[...] = added(y_send, y_buf)
        for i in FAR_FIRST:
            copy(z_send, z_buf.at[i - 1], ROW_Z + it, z_peer(i)).start()

    def turn(row):
        return jnp.transpose(jnp.broadcast_to(row, (128, 128)))

    def rows_end(it):
        _, _, z_send, z_buf = row_refs(it)
        got(z_buf, ROW_Z + it)
        total = added(z_send, z_buf)
        r = 1.0 / total[0:4, :]
        for j in range(4):
            rb[128 * j:128 * j + 128, :] = turn(r[j:j + 1, :])
        return total

    def column_pass():
        def body(i, acc):
            rows = pl.ds(pl.multiple_of(i * 8, 8), 8)
            r8 = rb[rows, :]
            return tuple(acc[q] + e_ref[rows, 128 * q:128 * q + 128] * r8 for q in range(16))

        acc = lax.fori_loop(0, 64, body, tuple(jnp.zeros((8, 128), F32) for _ in range(16)), unroll=4)
        for q in range(16):
            csum[q:q + 1, :] = jnp.sum(acc[q], axis=0, keepdims=True)

    def student_chunk(q, carry):
        w, at = chunk(q)
        inv = jnp.concatenate([ivec[pl.ds(2 * q, 1), :], ivec[pl.ds(2 * q + 1, 1), :]], axis=1)
        logits = jnp.dot(fs[...].reshape(512, 384), w, preferred_element_type=F32) * (inv * S_SCALE)
        l_ref[:, at] = logits
        p = jnp.exp2(logits)
        eacc[...] += p[:, :128] + p[:, 128:]
        pb[:, at] = (p * inv).astype(BF16)
        return carry

    def product(first, last):
        total = None
        for n in range(4):
            h, kk = divmod(n, 2)
            term = lax.dot_general(
                pb[:, 512 * n:512 * n + 512], wb[h, kk].reshape(384, 512)[first:last], NT, preferred_element_type=F32
            )
            total = term if total is None else total + term
        return total

    def gradient_a(dst):
        ga[...] = product(0, 256)
        for a in range(8):
            dst[a] = jnp.concatenate([ga[crops(a, b), :] for b in range(8)], axis=0).astype(BF16)

    def gradient_b(dst):
        gb[...] = product(256, 384)
        for b in range(8):
            dst[b] = jnp.concatenate([gb[crops(a, b), :] for a in range(8)], axis=0).astype(BF16)

    def spread_a(src, dst, sem):
        for i in FAR_FIRST:
            copy(src.at[lax.rem(a_me + i, 8)], dst.at[i - 1], sem, a_peer(i)).start()

    def spread_b(src, dst, sem):
        for i in FAR_FIRST:
            copy(src.at[lax.rem(b_me + i, 8)], dst.at[i - 1], sem, b_peer(i)).start()

    columns_start(0)
    lry_send[...] = jnp.zeros_like(lry_send)
    eacc[...] = jnp.zeros_like(eacc)
    loads[3].wait()
    col_cot[...] = turn(cot_ref[...])
    columns_end(0)
    row_pass()
    rows_start(0)
    rows_in(fs, S_Y)
    lax.fori_loop(0, 2, student_chunk, 0)
    rows_middle(0)
    lax.fori_loop(2, 5, student_chunk, 0)
    rows_end(0)
    column_pass()
    columns_start(1)
    lax.fori_loop(5, 8, student_chunk, 0)
    columns_end(1)
    row_pass()
    rows_start(1)
    gradient_a(g1a_send)
    rows_middle(1)
    spread_a(g1a_send, g1a_buf, G1_A)
    gradient_b(g1b_send)
    rows_end(1)
    spread_b(g1b_send, g1b_buf, G1_B)
    column_pass()
    columns_start(2)
    s16 = unit_rows(s_ref[...].astype(F32))
    s8, inv8 = (jnp.where(half == 0, v[0:8], v[8:16]) for v in s16)
    put(lry_send, 8, lanes(eacc))
    own_unit[...] = jnp.dot(s8, perm_ref[...].astype(F32), precision=HIGHEST, preferred_element_type=F32)
    columns_end(2)

    c_rows = [cvec[q:q + 1, :] for q in range(16)]
    i_rows = [ivec[q:q + 1, :] for q in range(16)]

    def last_pass(i, carry):
        rows = pl.ds(pl.multiple_of(i * 16, 16), 16)
        acc, acc2 = [], []
        for q in range(16):
            at = slice(128 * q, 128 * q + 128)
            v = e_ref[rows, at] * c_rows[q]
            acc.append(v)
            acc2.append(v * l_ref[rows, at])
            pb[rows, at] = (v * i_rows[q]).astype(BF16)
        rowacc[rows, :] = fold(acc)
        rowacc2[rows, :] = fold(acc2)
        return carry

    lax.fori_loop(0, 32, last_pass, 0, unroll=2)
    put(lry_send, 4, lanes(rowacc2))
    rows_start(2)
    gradient_a(g2a_send)
    spread_a(g2a_send, g2a_buf, G2_A)
    gradient_b(g2b_send)
    rows_middle(2)
    spread_b(g2b_send, g2b_buf, G2_B)

    def sum_blocks(own, buf):
        return fold([own.astype(F32)] + [buf[i].astype(F32) for i in range(7)])

    def wide(block, times):
        return jnp.concatenate([block] * times, axis=1)

    got(g1a_buf, G1_A)
    got(g1b_buf, G1_B)
    g1a = sum_blocks(g1a_send[a_me], g1a_buf)
    g1b = sum_blocks(g1b_send[b_me], g1b_buf)
    total = rows_end(2)
    vec[...] = total
    inv_total = 1.0 / total[8:12, :]
    for j in range(4):
        xb[128 * j:128 * j + 128, :] = turn(inv_total[j:j + 1, :])
    col_x[...] = turn(vec[pl.ds(lax.div(y, 2) + 4, 1), :])
    got(g2b_buf, G2_B)
    g2b = sum_blocks(g2b_send[b_me], g2b_buf)
    for a in range(8):
        rows, part = crops(a, b_me), slice(8 * a, 8 * a + 8)
        ub_send[a] = g1b[part] * xb[rows, :] - g2b[part] * rb[rows, :]
    for i in FAR_FIRST:
        copy(ub_send.at[lax.rem(a_me + i, 8)], ub_buf.at[i - 1], U_B, a_peer(i)).start()
    got(g2a_buf, G2_A)
    g2a = sum_blocks(g2a_send[a_me], g2a_buf)
    for b in range(8):
        rows, part = crops(a_me, b), slice(8 * b, 8 * b + 8)
        u = g1a[part] * wide(xb[rows, :], 2) - g2a[part] * wide(rb[rows, :], 2)
        ua_send[b] = jnp.concatenate([u[:, :128], u[:, 128:]], axis=0).astype(BF16)
    for i in FAR_FIRST:
        copy(ua_send.at[lax.rem(b_me + i, 8)], ua_buf.at[i - 1], U_A, b_peer(i)).start()

    rows8 = pl.ds(pl.multiple_of(y * 64 + z * 8, 8), 8)
    cross = rb[rows8, :] * col_x[pl.ds(pl.multiple_of(half * 64 + z * 8, 8), 8), :]
    loss8 = -jnp.log(xb[rows8, :]) - math.log(2.0) * cross
    cot8 = wide(col_cot[pl.ds(pl.multiple_of(k * 64 + y * 8, 8), 8), :], 3)
    got(ub_buf, U_B)
    u_b = added(ub_send.at[a_me], ub_buf)
    got(ua_buf, U_A)
    u_a = sum_blocks(ua_send[b_me], ua_buf)
    u8 = jnp.concatenate([u_a[:8], u_a[8:], u_b], axis=1) * (cot8 / 0.1)
    unit8 = own_unit[...]
    along = jnp.sum(unit8 * u8, axis=1, keepdims=True)
    result = ((u8 - unit8 * along) * inv8).astype(BF16)
    result = lax.dot_general(result, perm_ref[...], NT, preferred_element_type=F32)
    first = loss8.astype(BF16).astype(F32)
    loss8 = jnp.where(lax.broadcasted_iota(jnp.int32, (8, 128), 1) < 64, first, loss8 - first)
    low_rows, high_rows = result[:, :256], jnp.concatenate([result[:, 256:], loss8], axis=1)
    result = jnp.concatenate([low_rows, high_rows], axis=0).astype(BF16)
    fin_send[...] = result
    fin_buf[k, y] = result
    for i in FAR_FIRST:
        copy(fin_send, fin_buf.at[k, y], FIN, y_peer(i)).start()
    got(fin_buf.at[k, pl.ds(0, 7)], FIN)
    copy(fin_buf.at[k], fin_buf.at[k], FIN_CORE, core).start()
    got(fin_buf.at[1 - k], FIN_CORE)
    out = fin_buf[...].reshape(16, 16, 256).astype(F32)
    grad_ref[:, :256] = out[:, :8, :].reshape(128, 256)
    grad_ref[:, 256:] = out[:, 8:, :128].reshape(128, 128)
    losses = jnp.transpose(out[:, 8:, 128:].reshape(128, 128))
    loss_ref[...] = losses[0:1, :] + losses[64:65, :]

    sent(fz_buf.at[pl.ds(0, 7)], F_Z)
    for buf, at in ((ft, T_Y), (fs, S_Y)):
        sent(buf.at[pl.ds(0, 2)], at)
        sent(buf.at[y], at + 1)
        sent(buf.at[y], at + 2)
        sent(buf.at[pl.ds(0, 3)], at + 3)
    for h in range(2):
        at, own = RING + 10 * h, piece(h, x)
        sent(wz_buf.at[h, pl.ds(0, 7)], W_Z + h)
        for n in range(6):
            sent(own.at[low], at + n)
        for n in range(6, 10):
            sent(own, at + n)
    for it in range(3):
        sent(c_buf.at[it], COLS + it)
        _, y_buf, _, z_buf = row_refs(it)
        sent(y_buf, ROW_Y + it)
        sent(z_buf, ROW_Z + it)
    for buf, sem in (
        (g1a_buf, G1_A), (g1b_buf, G1_B), (g2a_buf, G2_A), (g2b_buf, G2_B), (ua_buf, U_A), (ub_buf, U_B),
        (fin_buf.at[k, pl.ds(0, 7)], FIN), (fin_buf.at[k], FIN_CORE),
    ):
        sent(buf, sem)


def shards(teacher, student, proto_weight, cotangent):
    vmem, hbm = pl.BlockSpec(memory_space=pltpu.VMEM), pl.BlockSpec(memory_space=pltpu.HBM)
    v = pltpu.VMEM
    operands = (teacher, student, proto_weight, cotangent.reshape(1, 128))
    grad, loss = pl.pallas_call(
        kernel,
        out_shape=(v((128, 384), F32), v((1, 128), F32)),
        in_specs=[hbm] * 4,
        out_specs=(vmem, vmem),
        scratch_shapes=[
            v((16, 384), BF16), v((16, 384), BF16), v((12, 8192), BF16), v((1, 128), F32), v((384, 384), BF16),
            v((768, 128), F32), v((2, 8, 48, 128), BF16), v((2, 8, 48, 128), BF16), v((8, 48, 128), F32),
            v((96, 512), F32), v((2, 2, 4, 96, 512), BF16),
            v((48, 128), BF16), v((8, 48, 128), BF16), v((8, 64, 384), BF16), v((8, 64, 384), BF16),
            v((512, 2048), F32), v((512, 2048), F32), v((512, 2048), BF16),
            v((512, 128), F32), v((512, 128), F32), v((512, 128), F32), v((512, 128), F32), v((512, 128), F32),
            v((16, 128), F32), v((16, 128), F32),
            v((3, 16, 128), BF16), v((3, 7, 16, 128), BF16),
            v((2, 4, 128), F32), v((2, 7, 4, 128), F32), v((2, 4, 128), F32), v((2, 7, 4, 128), F32),
            v((512, 256), F32), v((512, 128), F32),
            v((8, 64, 256), BF16), v((7, 64, 256), BF16), v((8, 64, 128), BF16), v((7, 64, 128), BF16),
            v((8, 64, 256), BF16), v((7, 64, 256), BF16), v((8, 64, 128), BF16), v((7, 64, 128), BF16),
            v((8, 16, 128), BF16), v((7, 16, 128), BF16), v((8, 8, 128), F32), v((7, 8, 128), F32),
            v((16, 128), F32), v((16, 128), F32), v((16, 128), F32), v((7, 16, 128), F32), v((16, 128), F32), v((7, 16, 128), F32),
            v((128, 128), F32), v((128, 128), F32), v((8, 384), F32),
            v((16, 256), BF16), v((2, 8, 16, 256), BF16),
            pltpu.SemaphoreType.DMA((4,)), pltpu.SemaphoreType.DMA((COUNT,)), pltpu.SemaphoreType.DMA((COUNT,)),
        ],
        compiler_params=pltpu.CompilerParams(
            collective_id=0, has_side_effects=True, vmem_limit_bytes=60 * 1024 * 1024
        ),
        cost_estimate=pl.CostEstimate(flops=2_400_000_000, bytes_accessed=4_000_000, transcendentals=2_000_000),
    )(*(pltpu.with_memory_space_constraint(a, pltpu.HBM) for a in operands))
    return loss.reshape(128), grad


def solution(mesh):
    return jax.shard_map(
        shards,
        mesh=mesh,
        in_specs=(P("dp", None), P("dp", None), P("dp", "proto"), P("dp")),
        out_specs=(P("dp"), P("dp", None)),
        check_vma=False,
    )
```

```python
import math

import jax
import jax.numpy as jnp
from jax import lax
from jax.experimental import pallas as pl
from jax.experimental.pallas import tpu as pltpu
from jax.sharding import PartitionSpec as P

EPS = 1e-06
LOG2E = math.log2(math.e)
T_SCALE = LOG2E / 0.04
S_SCALE = LOG2E / 0.1
F32, BF16 = jnp.float32, jnp.bfloat16
MESH = pl.DeviceIdType.MESH
HIGHEST = lax.Precision.HIGHEST
NT = (((1,), (1,)), ((), ()))

FAR_FIRST = (4, 3, 5, 2, 6, 1, 7)

F_Z, W_Z = 0, 1
RING = 4
COLS = 24
ROW_Y, ROW_Z = 27, 30
G1, G2 = 33, 36
U_A, U_B, FIN = 39, 40, 41
T_Y, S_Y = 42, 46
COUNT = 50


def unit_rows(values):
    inv = lax.rsqrt(jnp.sum(values * values, axis=1, keepdims=True) + EPS)
    return values * inv, inv


def fold(terms):
    while len(terms) > 1:
        terms = [a + b for a, b in zip(terms[::2], terms[1::2])]
    return terms[0]


def kernel(
    t_hbm, s_hbm, w_hbm, cot_hbm,
    grad_ref, loss_ref,
    t_ref, s_ref, w_ref, cot_ref, perm_ref,
    pack, wz_send, wz_buf, wz_wide, asm, wb,
    fz_send, fz_buf, ft, fs,
    e_ref, l_ref, pb, rowacc, rowacc2, eacc, rb, xb, ivec, cvec,
    c_send, c_buf, ry_send, ry_buf, rz_send, rz_buf,
    gs, g1_send, g1_buf, g2_send, g2_buf,
    ua_send, ua_buf, ub_send, ub_buf, csum, vec, lry_send, lry_buf, lrz_send, lrz_buf,
    col_cot, col_x, own_unit,
    fin_send, fin_buf,
    lsem, ssem, rsem,
):
    dp, pr = lax.axis_index("dp"), lax.axis_index("proto")
    z, x = lax.div(dp, 4), lax.rem(dp, 4)
    y, k = lax.div(pr, 2), lax.rem(pr, 2)

    def z_peer(i):
        return (lax.rem(z + i, 8) * 4 + x, pr)

    def y_peer(i):
        return (dp, lax.rem(y + i, 8) * 2 + k)

    def xk_peer(i):
        g = lax.rem(x * 2 + k + i, 8)
        return (z * 4 + lax.div(g, 2), y * 2 + lax.rem(g, 2))

    def y_cross(i):
        return (dp, lax.rem(y + i, 8) * 2 + 1 - k)

    def a_peer(i):
        y_at, z_at = y_peer(i)[1], z_peer(i)[0]
        return (dp + k * (z_at - dp), y_at + k * (pr - y_at))

    def b_peer(i):
        y_at, z_at = y_peer(i)[1], z_peer(i)[0]
        return (z_at + k * (dp - z_at), pr + k * (y_at - pr))

    a_me, b_me = y + k * (z - y), z + k * (y - z)
    a_step, b_step = 64 - 56 * k, 8 + 56 * k

    def crops(a, b):
        return pl.ds(pl.multiple_of(a * a_step + b * b_step, 8), 8)

    def copy(src, dst, sem, peer):
        return pltpu.make_async_remote_copy(
            src_ref=src, dst_ref=dst, send_sem=ssem.at[sem], recv_sem=rsem.at[sem],
            device_id=peer, device_id_type=MESH,
        )

    def got(ref, sem):
        copy(ref, ref, sem, (dp, pr)).wait_recv()

    def sent(ref, sem):
        copy(ref, ref, sem, (dp, pr)).wait_send()

    half = lax.rem(y, 2)
    at16 = pl.multiple_of(k * 64 + lax.div(y, 2) * 16, 16)
    rows16 = pl.ds(at16, 16)
    loads = [
        pltpu.make_async_copy(src, dst, lsem.at[n])
        for n, (src, dst) in enumerate((
            (w_hbm, w_ref), (t_hbm.at[rows16], t_ref), (s_hbm.at[rows16], s_ref), (cot_hbm, cot_ref)
        ))
    ]
    for load in loads:
        load.start()

    barrier = pltpu.get_barrier_semaphore()
    for i in range(1, 8):
        for peer in (z_peer(i), y_peer(i), xk_peer(i), y_cross(i)):
            pl.semaphore_signal(barrier, inc=1, device_id=peer, device_id_type=MESH)

    feature = lax.broadcasted_iota(jnp.int32, (384, 128), 0)
    fz = lax.shift_right_logical(feature * 1366, 16)
    fx = lax.shift_right_logical((feature - fz * 48) * 5462, 16)
    place = fx * 96 + fz * 12 + (feature - fz * 48 - fx * 12)
    lane = lax.broadcasted_iota(jnp.int32, (384, 128), 1)
    for n in range(3):
        perm_ref[:, 128 * n:128 * n + 128] = (place == lane + 128 * n).astype(F32).astype(BF16)

    loads[0].wait()
    for d in range(8):
        for h in range(2):
            for r in range(4):
                q, at = d * 8 + h * 4 + r, ((h * 8 + d) * 4 + r) * 12
                pack[at:at + 12, :] = w_ref[:, 128 * q:128 * q + 128].astype(F32)
    for h in range(2):
        for d in range(8):
            at = (h * 8 + d) * 48
            wz_send[h, d] = pack[at:at + 48, :].astype(BF16)
        wz_buf[h, z] = wz_send[h, z]

    pl.semaphore_wait(barrier, 28)

    def weights_out(h):
        for i in FAR_FIRST:
            copy(wz_send.at[h, lax.rem(z + i, 8)], wz_buf.at[h, z], W_Z + h, z_peer(i)).start()

    weights_out(0)
    loads[1].wait()
    loads[2].wait()
    v = jnp.concatenate([t_ref[...].astype(F32), s_ref[...].astype(F32)], axis=0)
    v = jnp.dot(unit_rows(v)[0].astype(BF16), perm_ref[...], preferred_element_type=F32)
    v = [jnp.where(half == 0, v[at:at + 8], v[at + 8:at + 16]) for at in (0, 16)]
    v = jnp.concatenate([m[:, 128 * n:128 * n + 128] for m in v for n in range(3)], axis=0).astype(BF16)
    fz_send[...] = v
    fz_buf[z] = v
    for i in FAR_FIRST:
        copy(fz_send, fz_buf.at[z], F_Z, z_peer(i)).start()
    weights_out(1)

    first, second = pl.ds(0, 32), pl.ds(32, 32)

    def rows_out(buf, at):
        block = buf.at[y]
        copy(block, block, at + 1, y_peer(2)).start()
        copy(block, block, at + 2, y_peer(6)).start()
        copy(block, block, at, y_peer(1)).start()
        copy(block, block, at, y_peer(7)).start()

    def rows_on(buf, at):
        below, above = buf.at[lax.rem(y + 6, 8)], buf.at[lax.rem(y + 2, 8)]
        got(below, at + 1)
        copy(below.at[first], below.at[first], at + 3, y_peer(2)).start()
        copy(below, below, at + 3, y_peer(1)).start()
        got(above, at + 2)
        copy(above.at[second], above.at[second], at + 3, y_peer(6)).start()
        copy(above, above, at + 3, y_peer(7)).start()

    def rows_in(buf, at):
        got(buf.at[pl.ds(0, 2)], at)
        got(buf.at[pl.ds(0, 3)], at + 3)

    x_right, x_left, x_far = lax.rem(x + 1, 4), lax.rem(x + 3, 4), lax.rem(x + 2, 4)
    right, left, core = (z * 4 + x_right, pr), (z * 4 + x_left, pr), (dp, y * 2 + 1 - k)
    low, high = pl.ds(0, 48), pl.ds(48, 48)

    def piece(h, at):
        return wb.at[h, k, at]

    for h in range(2):
        got(wz_buf.at[h, pl.ds(0, 7)], W_Z + h)
        for s in range(8):
            wz_wide[s] = wz_buf[h, s].astype(F32)
            for q in range(4):
                asm[12 * s:12 * s + 12, 128 * q:128 * q + 128] = wz_wide[s, 12 * q:12 * q + 12, :]
        wb[h, k, x] = asm[...].astype(BF16)
        own = piece(h, x)
        at = RING + 10 * h
        copy(own.at[low], own.at[low], at, right).start()
        copy(own.at[high], own.at[high], at + 2, left).start()
        copy(own.at[high], own.at[high], at + 1, right).start()
        copy(own.at[low], own.at[low], at + 3, left).start()
        copy(own, own, at + 6, core).start()
        if h == 0:
            got(fz_buf.at[pl.ds(0, 7)], F_Z)
            for buf, at in ((ft, 0), (fs, 24)):
                v = [fz_buf[d, :, :].astype(F32) for d in range(8)]
                v = [jnp.concatenate([m[at + 8 * n:at + 8 * n + 8] for m in v], axis=0) for n in range(3)]
                buf[y] = jnp.concatenate(v, axis=1).astype(BF16)
            rows_out(ft, T_Y)
        else:
            rows_on(ft, T_Y)
            rows_out(fs, S_Y)

    def relay(h):
        at, from_left, from_right = RING + 10 * h, piece(h, x_left), piece(h, x_right)
        got(from_left.at[low], at)
        copy(from_left.at[low], from_left.at[low], at + 4, right).start()
        got(from_right.at[high], at + 2)
        copy(from_right.at[high], from_right.at[high], at + 5, left).start()
        got(from_left.at[high], at + 1)
        copy(from_left, from_left, at + 7, core).start()
        got(from_right.at[low], at + 3)
        copy(from_right, from_right, at + 8, core).start()

    def far_piece(h):
        far = piece(h, x_far)
        got(far.at[low], RING + 10 * h + 4)
        got(far.at[high], RING + 10 * h + 5)
        copy(far, far, RING + 10 * h + 9, core).start()

    relay(0)
    far_piece(0)
    relay(1)
    rows_in(ft, T_Y)

    def chunk(q):
        h, kk, c0 = lax.div(q, 4), lax.rem(lax.div(q, 2), 2), pl.multiple_of(lax.rem(q, 2) * 256, 256)
        return wb[h, kk, :, :, pl.ds(c0, 256)].reshape(384, 256), pl.ds(pl.multiple_of(q * 256, 256), 256)

    def teacher_chunk(q, carry):
        w, at = chunk(q)
        wf = w.astype(F32)
        inv = lax.rsqrt(jnp.sum(wf * wf, axis=0, keepdims=True) + EPS)
        scores = jnp.dot(ft[...].reshape(512, 384), w, preferred_element_type=F32)
        e = jnp.exp2(scores * (inv * T_SCALE))
        e_ref[:, at] = e
        col = jnp.sum(e, axis=0, keepdims=True)
        for n in range(2):
            part = slice(128 * n, 128 * n + 128)
            ivec[pl.ds(2 * q + n, 1), :] = inv[:, part]
            csum[pl.ds(2 * q + n, 1), :] = col[:, part]
        return carry

    def teacher_part(h, kk):
        lax.fori_loop(0, 2, lambda c, carry: teacher_chunk(4 * h + 2 * kk + c, carry), 0)

    for h in range(2):
        if h == 1:
            far_piece(1)
        teacher_part(h, k)
        if h == 1:
            rows_on(fs, S_Y)
        for n in range(4):
            got(piece(h, x), RING + 10 * h + 6 + n)
        teacher_part(h, 1 - k)

    def columns_start(it):
        c_send[it] = csum[...].astype(BF16)
        for i in FAR_FIRST:
            copy(c_send.at[it], c_buf.at[it, i - 1], COLS + it, xk_peer(i)).start()

    def columns_end(it):
        got(c_buf.at[it], COLS + it)
        cvec[...] = 1.0 / fold([c_send[it].astype(F32)] + [c_buf[it, i].astype(F32) for i in range(7)])

    def row_pass():
        scale = [cvec[q:q + 1, :] for q in range(16)]

        def body(i, carry):
            rows = pl.ds(pl.multiple_of(i * 16, 16), 16)
            rowacc[rows, :] = fold([e_ref[rows, 128 * q:128 * q + 128] * scale[q] for q in range(16)])
            return carry

        lax.fori_loop(0, 32, body, 0, unroll=4)

    def lanes(ref):
        return [jnp.sum(jnp.transpose(ref[128 * j:128 * j + 128, :]), axis=0, keepdims=True) for j in range(4)]

    def put(dst, at, sums):
        for j in range(4):
            dst[at + j:at + j + 1, :] = sums[j]

    def row_refs(it):
        if it == 2:
            return lry_send, lry_buf, lrz_send, lrz_buf
        return ry_send.at[it], ry_buf.at[it], rz_send.at[it], rz_buf.at[it]

    def added(own, buf):
        return fold([own[...]] + [buf[i] for i in range(7)])

    def rows_start(it):
        y_send, y_buf, _, _ = row_refs(it)
        put(y_send, 0, lanes(rowacc))
        for i in FAR_FIRST:
            copy(y_send, y_buf.at[i - 1], ROW_Y + it, y_peer(i)).start()

    def rows_middle(it):
        y_send, y_buf, z_send, z_buf = row_refs(it)
        got(y_buf, ROW_Y + it)
        z_send[...] = added(y_send, y_buf)
        for i in FAR_FIRST:
            copy(z_send, z_buf.at[i - 1], ROW_Z + it, z_peer(i)).start()

    def turn(row):
        return jnp.transpose(jnp.broadcast_to(row, (128, 128)))

    def rows_end(it):
        _, _, z_send, z_buf = row_refs(it)
        got(z_buf, ROW_Z + it)
        total = added(z_send, z_buf)
        r = 1.0 / total[0:4, :]
        for j in range(4):
            rb[128 * j:128 * j + 128, :] = turn(r[j:j + 1, :])
        return total

    def column_pass():
        def body(i, acc):
            rows = pl.ds(pl.multiple_of(i * 8, 8), 8)
            r8 = rb[rows, :]
            return tuple(acc[q] + e_ref[rows, 128 * q:128 * q + 128] * r8 for q in range(16))

        acc = lax.fori_loop(0, 64, body, tuple(jnp.zeros((8, 128), F32) for _ in range(16)), unroll=4)
        for q in range(16):
            csum[q:q + 1, :] = jnp.sum(acc[q], axis=0, keepdims=True)

    def student_chunk(q, carry):
        w, at = chunk(q)
        inv = jnp.concatenate([ivec[pl.ds(2 * q, 1), :], ivec[pl.ds(2 * q + 1, 1), :]], axis=1)
        logits = jnp.dot(fs[...].reshape(512, 384), w, preferred_element_type=F32) * (inv * S_SCALE)
        l_ref[:, at] = logits
        p = jnp.exp2(logits)
        eacc[...] += p[:, :128] + p[:, 128:]
        pb[:, at] = (p * inv).astype(BF16)
        return carry

    def product(first, last):
        total = None
        for n in range(4):
            h, kk = divmod(n, 2)
            term = lax.dot_general(
                pb[:, 512 * n:512 * n + 512], wb[h, kk].reshape(384, 512)[first:last], NT, preferred_element_type=F32
            )
            total = term if total is None else total + term
        return total

    def gradient(p, dst):
        gs[...] = product(128 * p, 128 * p + 128)
        for i in range(8):
            at = [crops(i, j) if p < 2 else crops(j, i) for j in range(8)]
            dst[p, i] = jnp.concatenate([gs[rows, :] for rows in at], axis=0).astype(BF16)

    def spread(p, src, dst, sem):
        me, peer = (a_me, a_peer) if p < 2 else (b_me, b_peer)
        for i in FAR_FIRST:
            copy(src.at[p, lax.rem(me + i, 8)], dst.at[p, i - 1], sem + p, peer(i)).start()

    def gathered(p, src, dst, sem):
        got(dst.at[p], sem + p)
        own = src[p, a_me if p < 2 else b_me]
        return fold([own.astype(F32)] + [dst[p, i].astype(F32) for i in range(7)])

    columns_start(0)
    lry_send[...] = jnp.zeros_like(lry_send)
    eacc[...] = jnp.zeros_like(eacc)
    loads[3].wait()
    col_cot[...] = turn(cot_ref[...])
    columns_end(0)
    row_pass()
    rows_start(0)
    rows_in(fs, S_Y)
    lax.fori_loop(0, 2, student_chunk, 0)
    rows_middle(0)
    lax.fori_loop(2, 5, student_chunk, 0)
    rows_end(0)
    column_pass()
    columns_start(1)
    lax.fori_loop(5, 8, student_chunk, 0)
    columns_end(1)
    row_pass()
    rows_start(1)
    gradient(0, g1_send)
    gradient(1, g1_send)
    rows_middle(1)
    spread(0, g1_send, g1_buf, G1)
    spread(1, g1_send, g1_buf, G1)
    gradient(2, g1_send)
    rows_end(1)
    spread(2, g1_send, g1_buf, G1)
    column_pass()
    columns_start(2)
    s16 = unit_rows(s_ref[...].astype(F32))
    s8, inv8 = (jnp.where(half == 0, v[0:8], v[8:16]) for v in s16)
    put(lry_send, 8, lanes(eacc))
    own_unit[...] = jnp.dot(s8, perm_ref[...].astype(F32), precision=HIGHEST, preferred_element_type=F32)
    columns_end(2)

    c_rows = [cvec[q:q + 1, :] for q in range(16)]
    i_rows = [ivec[q:q + 1, :] for q in range(16)]

    def last_pass(i, carry):
        rows = pl.ds(pl.multiple_of(i * 16, 16), 16)
        acc, acc2 = [], []
        for q in range(16):
            at = slice(128 * q, 128 * q + 128)
            v = e_ref[rows, at] * c_rows[q]
            acc.append(v)
            acc2.append(v * l_ref[rows, at])
            pb[rows, at] = (v * i_rows[q]).astype(BF16)
        rowacc[rows, :] = fold(acc)
        rowacc2[rows, :] = fold(acc2)
        return carry

    lax.fori_loop(0, 32, last_pass, 0, unroll=2)
    put(lry_send, 4, lanes(rowacc2))
    rows_start(2)
    gradient(0, g2_send)
    spread(0, g2_send, g2_buf, G2)
    gradient(2, g2_send)
    spread(2, g2_send, g2_buf, G2)
    rows_middle(2)
    gradient(1, g2_send)
    spread(1, g2_send, g2_buf, G2)

    def sum_blocks(own, buf):
        return fold([own.astype(F32)] + [buf[i].astype(F32) for i in range(7)])

    def wide(block, times):
        return jnp.concatenate([block] * times, axis=1)

    g1 = [gathered(p, g1_send, g1_buf, G1) for p in range(3)]
    total = rows_end(2)
    vec[...] = total
    inv_total = 1.0 / total[8:12, :]
    for j in range(4):
        xb[128 * j:128 * j + 128, :] = turn(inv_total[j:j + 1, :])
    col_x[...] = turn(vec[pl.ds(lax.div(y, 2) + 4, 1), :])
    g2b = gathered(2, g2_send, g2_buf, G2)
    for a in range(8):
        rows, part = crops(a, b_me), slice(8 * a, 8 * a + 8)
        ub_send[a] = g1[2][part] * xb[rows, :] - g2b[part] * rb[rows, :]
    for i in FAR_FIRST:
        copy(ub_send.at[lax.rem(a_me + i, 8)], ub_buf.at[i - 1], U_B, a_peer(i)).start()
    g2a = [gathered(p, g2_send, g2_buf, G2) for p in range(2)]
    for b in range(8):
        rows, part = crops(a_me, b), slice(8 * b, 8 * b + 8)
        u = [g1[p][part] * xb[rows, :] - g2a[p][part] * rb[rows, :] for p in range(2)]
        ua_send[b] = jnp.concatenate(u, axis=0).astype(BF16)
    for i in FAR_FIRST:
        copy(ua_send.at[lax.rem(b_me + i, 8)], ua_buf.at[i - 1], U_A, b_peer(i)).start()

    rows8 = pl.ds(pl.multiple_of(y * 64 + z * 8, 8), 8)
    cross = rb[rows8, :] * col_x[pl.ds(pl.multiple_of(half * 64 + z * 8, 8), 8), :]
    loss8 = -jnp.log(xb[rows8, :]) - math.log(2.0) * cross
    cot8 = wide(col_cot[pl.ds(pl.multiple_of(k * 64 + y * 8, 8), 8), :], 3)
    got(ub_buf, U_B)
    u_b = added(ub_send.at[a_me], ub_buf)
    got(ua_buf, U_A)
    u_a = sum_blocks(ua_send[b_me], ua_buf)
    u8 = jnp.concatenate([u_a[:8], u_a[8:], u_b], axis=1) * (cot8 / 0.1)
    unit8 = own_unit[...]
    along = jnp.sum(unit8 * u8, axis=1, keepdims=True)
    result = ((u8 - unit8 * along) * inv8).astype(BF16)
    result = lax.dot_general(result, perm_ref[...], NT, preferred_element_type=F32)
    first = loss8.astype(BF16).astype(F32)
    loss8 = jnp.where(lax.broadcasted_iota(jnp.int32, (8, 128), 1) < 64, first, loss8 - first)
    low_rows, high_rows = result[:, :256], jnp.concatenate([result[:, 256:], loss8], axis=1)
    result = jnp.concatenate([low_rows, high_rows], axis=0).astype(BF16)
    fin_send[...] = result
    slot = k * 8 + y
    fin_buf[slot] = result
    for i in FAR_FIRST:
        copy(fin_send, fin_buf.at[slot], FIN, y_peer(i)).start()
        copy(fin_send, fin_buf.at[slot], FIN, y_cross(i)).start()
    copy(fin_send, fin_buf.at[slot], FIN, core).start()
    got(fin_buf.at[pl.ds(0, 15)], FIN)
    out = fin_buf[...].astype(F32)
    grad_ref[:, :256] = out[:, :8, :].reshape(128, 256)
    grad_ref[:, 256:] = out[:, 8:, :128].reshape(128, 128)
    losses = jnp.transpose(out[:, 8:, 128:].reshape(128, 128))
    loss_ref[...] = losses[0:1, :] + losses[64:65, :]

    sent(fz_buf.at[pl.ds(0, 7)], F_Z)
    for buf, at in ((ft, T_Y), (fs, S_Y)):
        sent(buf.at[pl.ds(0, 2)], at)
        sent(buf.at[y], at + 1)
        sent(buf.at[y], at + 2)
        sent(buf.at[pl.ds(0, 3)], at + 3)
    for h in range(2):
        at, own = RING + 10 * h, piece(h, x)
        sent(wz_buf.at[h, pl.ds(0, 7)], W_Z + h)
        for n in range(6):
            sent(own.at[low], at + n)
        for n in range(6, 10):
            sent(own, at + n)
    for it in range(3):
        sent(c_buf.at[it], COLS + it)
        _, y_buf, _, z_buf = row_refs(it)
        sent(y_buf, ROW_Y + it)
        sent(z_buf, ROW_Z + it)
    for p in range(3):
        sent(g1_buf.at[p], G1 + p)
        sent(g2_buf.at[p], G2 + p)
    for buf, sem in (
        (ua_buf, U_A), (ub_buf, U_B),
        (fin_buf.at[pl.ds(0, 15)], FIN),
    ):
        sent(buf, sem)


def shards(teacher, student, proto_weight, cotangent):
    vmem, hbm = pl.BlockSpec(memory_space=pltpu.VMEM), pl.BlockSpec(memory_space=pltpu.HBM)
    v = pltpu.VMEM
    operands = (teacher, student, proto_weight, cotangent.reshape(1, 128))
    grad, loss = pl.pallas_call(
        kernel,
        out_shape=(v((128, 384), F32), v((1, 128), F32)),
        in_specs=[hbm] * 4,
        out_specs=(vmem, vmem),
        scratch_shapes=[
            v((16, 384), BF16), v((16, 384), BF16), v((12, 8192), BF16), v((1, 128), F32), v((384, 384), BF16),
            v((768, 128), F32), v((2, 8, 48, 128), BF16), v((2, 8, 48, 128), BF16), v((8, 48, 128), F32),
            v((96, 512), F32), v((2, 2, 4, 96, 512), BF16),
            v((48, 128), BF16), v((8, 48, 128), BF16), v((8, 64, 384), BF16), v((8, 64, 384), BF16),
            v((512, 2048), F32), v((512, 2048), F32), v((512, 2048), BF16),
            v((512, 128), F32), v((512, 128), F32), v((512, 128), F32), v((512, 128), F32), v((512, 128), F32),
            v((16, 128), F32), v((16, 128), F32),
            v((3, 16, 128), BF16), v((3, 7, 16, 128), BF16),
            v((2, 4, 128), F32), v((2, 7, 4, 128), F32), v((2, 4, 128), F32), v((2, 7, 4, 128), F32),
            v((512, 128), F32),
            v((3, 8, 64, 128), BF16), v((3, 7, 64, 128), BF16), v((3, 8, 64, 128), BF16), v((3, 7, 64, 128), BF16),
            v((8, 16, 128), BF16), v((7, 16, 128), BF16), v((8, 8, 128), F32), v((7, 8, 128), F32),
            v((16, 128), F32), v((16, 128), F32), v((16, 128), F32), v((7, 16, 128), F32), v((16, 128), F32), v((7, 16, 128), F32),
            v((128, 128), F32), v((128, 128), F32), v((8, 384), F32),
            v((16, 256), BF16), v((16, 16, 256), BF16),
            pltpu.SemaphoreType.DMA((4,)), pltpu.SemaphoreType.DMA((COUNT,)), pltpu.SemaphoreType.DMA((COUNT,)),
        ],
        compiler_params=pltpu.CompilerParams(
            collective_id=0, has_side_effects=True, vmem_limit_bytes=60 * 1024 * 1024
        ),
        cost_estimate=pl.CostEstimate(flops=2_400_000_000, bytes_accessed=4_000_000, transcendentals=2_000_000),
    )(*(pltpu.with_memory_space_constraint(a, pltpu.HBM) for a in operands))
    return loss.reshape(128), grad


def solution(mesh):
    return jax.shard_map(
        shards,
        mesh=mesh,
        in_specs=(P("dp", None), P("dp", None), P("dp", "proto"), P("dp")),
        out_specs=(P("dp"), P("dp", None)),
        check_vma=False,
    )
```

```python
import math

import jax
import jax.numpy as jnp
from jax import lax
from jax.experimental import pallas as pl
from jax.experimental.pallas import tpu as pltpu
from jax.sharding import PartitionSpec as P

EPS = 1e-06
LOG2E = math.log2(math.e)
T_SCALE = LOG2E / 0.04
S_SCALE = LOG2E / 0.1
F32, BF16 = jnp.float32, jnp.bfloat16
MESH = pl.DeviceIdType.MESH
HIGHEST = lax.Precision.HIGHEST
NT = (((1,), (1,)), ((), ()))

FAR_FIRST = (4, 3, 5, 2, 6, 1, 7)

F_Z, W_Z = 0, 1
RING = 4
COLS = 24
ROW_Y, ROW_Z = 27, 30
G1, G2 = 33, 36
U_A, U_B, FIN = 39, 40, 41
T_Y, S_Y = 42, 46
COUNT = 50


def unit_rows(values):
    inv = lax.rsqrt(jnp.sum(values * values, axis=1, keepdims=True) + EPS)
    return values * inv, inv


def fold(terms):
    while len(terms) > 1:
        terms = [a + b for a, b in zip(terms[::2], terms[1::2])]
    return terms[0]


def kernel(
    t_hbm, s_hbm, w_hbm, cot_hbm,
    grad_ref, loss_ref,
    t_ref, s_ref, w_ref, cot_ref, perm_ref,
    pack, wz_send, wz_buf, wz_wide, asm, wb,
    fz_send, fz_buf, ft, fs,
    e_ref, l_ref, pb, rowacc, rowacc2, eacc, rb, xb, ivec, cvec,
    c_send, c_buf, ry_send, ry_buf, rz_send, rz_buf,
    gs, g1_send, g1_buf, g2_send, g2_buf,
    ua_send, ua_buf, ub_send, ub_buf, csum, vec, lry_send, lry_buf, lrz_send, lrz_buf,
    col_cot, col_x, own_unit,
    fin_send, fin_buf,
    lsem, ssem, rsem,
):
    dp, pr = lax.axis_index("dp"), lax.axis_index("proto")
    z, x = lax.div(dp, 4), lax.rem(dp, 4)
    y, k = lax.div(pr, 2), lax.rem(pr, 2)

    def z_peer(i):
        return (lax.rem(z + i, 8) * 4 + x, pr)

    def y_peer(i):
        return (dp, lax.rem(y + i, 8) * 2 + k)

    def xk_peer(i):
        g = lax.rem(x * 2 + k + i, 8)
        return (z * 4 + lax.div(g, 2), y * 2 + lax.rem(g, 2))

    def y_cross(i):
        return (dp, lax.rem(y + i, 8) * 2 + 1 - k)

    def a_peer(i):
        y_at, z_at = y_peer(i)[1], z_peer(i)[0]
        return (dp + k * (z_at - dp), y_at + k * (pr - y_at))

    def b_peer(i):
        y_at, z_at = y_peer(i)[1], z_peer(i)[0]
        return (z_at + k * (dp - z_at), pr + k * (y_at - pr))

    a_me, b_me = y + k * (z - y), z + k * (y - z)
    a_step, b_step = 64 - 56 * k, 8 + 56 * k

    def crops(a, b):
        return pl.ds(pl.multiple_of(a * a_step + b * b_step, 8), 8)

    def copy(src, dst, sem, peer):
        return pltpu.make_async_remote_copy(
            src_ref=src, dst_ref=dst, send_sem=ssem.at[sem], recv_sem=rsem.at[sem],
            device_id=peer, device_id_type=MESH,
        )

    def got(ref, sem):
        copy(ref, ref, sem, (dp, pr)).wait_recv()

    def sent(ref, sem):
        copy(ref, ref, sem, (dp, pr)).wait_send()

    half = lax.rem(y, 2)
    at16 = pl.multiple_of(k * 64 + lax.div(y, 2) * 16, 16)
    rows16 = pl.ds(at16, 16)
    loads = [
        pltpu.make_async_copy(src, dst, lsem.at[n])
        for n, (src, dst) in enumerate((
            (w_hbm, w_ref), (t_hbm.at[rows16], t_ref), (s_hbm.at[rows16], s_ref), (cot_hbm, cot_ref)
        ))
    ]
    for load in loads:
        load.start()

    barrier = pltpu.get_barrier_semaphore()
    for i in range(1, 8):
        for peer in (z_peer(i), y_peer(i), xk_peer(i), y_cross(i)):
            pl.semaphore_signal(barrier, inc=1, device_id=peer, device_id_type=MESH)

    feature = lax.broadcasted_iota(jnp.int32, (384, 128), 0)
    fz = lax.shift_right_logical(feature * 1366, 16)
    fx = lax.shift_right_logical((feature - fz * 48) * 5462, 16)
    place = fx * 96 + fz * 12 + (feature - fz * 48 - fx * 12)
    lane = lax.broadcasted_iota(jnp.int32, (384, 128), 1)
    for n in range(3):
        perm_ref[:, 128 * n:128 * n + 128] = (place == lane + 128 * n).astype(F32).astype(BF16)

    loads[0].wait()
    for d in range(8):
        for h in range(2):
            for r in range(4):
                q, at = d * 8 + h * 4 + r, ((h * 8 + d) * 4 + r) * 12
                pack[at:at + 12, :] = w_ref[:, 128 * q:128 * q + 128].astype(F32)
    for h in range(2):
        for d in range(8):
            at = (h * 8 + d) * 48
            wz_send[h, d] = pack[at:at + 48, :].astype(BF16)
        wz_buf[h, z] = wz_send[h, z]

    pl.semaphore_wait(barrier, 28)

    def weights_out(h):
        for i in FAR_FIRST:
            copy(wz_send.at[h, lax.rem(z + i, 8)], wz_buf.at[h, z], W_Z + h, z_peer(i)).start()

    weights_out(0)
    loads[1].wait()
    loads[2].wait()
    v = jnp.concatenate([t_ref[...].astype(F32), s_ref[...].astype(F32)], axis=0)
    v = jnp.dot(unit_rows(v)[0].astype(BF16), perm_ref[...], preferred_element_type=F32)
    v = [jnp.where(half == 0, v[at:at + 8], v[at + 8:at + 16]) for at in (0, 16)]
    v = jnp.concatenate([m[:, 128 * n:128 * n + 128] for m in v for n in range(3)], axis=0).astype(BF16)
    fz_send[...] = v
    fz_buf[z] = v
    for i in FAR_FIRST:
        copy(fz_send, fz_buf.at[z], F_Z, z_peer(i)).start()
    weights_out(1)

    first, second = pl.ds(0, 32), pl.ds(32, 32)

    def rows_out(buf, at):
        block = buf.at[y]
        copy(block, block, at + 1, y_peer(2)).start()
        copy(block, block, at + 2, y_peer(6)).start()
        copy(block, block, at, y_peer(1)).start()
        copy(block, block, at, y_peer(7)).start()

    def rows_on(buf, at):
        below, above = buf.at[lax.rem(y + 6, 8)], buf.at[lax.rem(y + 2, 8)]
        got(below, at + 1)
        copy(below.at[first], below.at[first], at + 3, y_peer(2)).start()
        copy(below, below, at + 3, y_peer(1)).start()
        got(above, at + 2)
        copy(above.at[second], above.at[second], at + 3, y_peer(6)).start()
        copy(above, above, at + 3, y_peer(7)).start()

    def rows_in(buf, at):
        got(buf.at[pl.ds(0, 2)], at)
        got(buf.at[pl.ds(0, 3)], at + 3)

    x_right, x_left, x_far = lax.rem(x + 1, 4), lax.rem(x + 3, 4), lax.rem(x + 2, 4)
    right, left, core = (z * 4 + x_right, pr), (z * 4 + x_left, pr), (dp, y * 2 + 1 - k)
    low, high = pl.ds(0, 48), pl.ds(48, 48)

    def piece(h, at):
        return wb.at[h, k, at]

    for h in range(2):
        got(wz_buf.at[h, pl.ds(0, 7)], W_Z + h)
        for s in range(8):
            wz_wide[s] = wz_buf[h, s].astype(F32)
            for q in range(4):
                asm[12 * s:12 * s + 12, 128 * q:128 * q + 128] = wz_wide[s, 12 * q:12 * q + 12, :]
        wb[h, k, x] = asm[...].astype(BF16)
        own = piece(h, x)
        at = RING + 10 * h
        copy(own.at[low], own.at[low], at, right).start()
        copy(own.at[high], own.at[high], at + 2, left).start()
        copy(own.at[high], own.at[high], at + 1, right).start()
        copy(own.at[low], own.at[low], at + 3, left).start()
        copy(own, own, at + 6, core).start()
        if h == 0:
            got(fz_buf.at[pl.ds(0, 7)], F_Z)
            for buf, at in ((ft, 0), (fs, 24)):
                v = [fz_buf[d, :, :].astype(F32) for d in range(8)]
                v = [jnp.concatenate([m[at + 8 * n:at + 8 * n + 8] for m in v], axis=0) for n in range(3)]
                buf[y] = jnp.concatenate(v, axis=1).astype(BF16)
            rows_out(ft, T_Y)
        else:
            rows_on(ft, T_Y)
            rows_out(fs, S_Y)

    def relay(h):
        at, from_left, from_right = RING + 10 * h, piece(h, x_left), piece(h, x_right)
        got(from_left.at[low], at)
        copy(from_left.at[low], from_left.at[low], at + 4, right).start()
        got(from_right.at[high], at + 2)
        copy(from_right.at[high], from_right.at[high], at + 5, left).start()
        got(from_left.at[high], at + 1)
        copy(from_left, from_left, at + 7, core).start()
        got(from_right.at[low], at + 3)
        copy(from_right, from_right, at + 8, core).start()

    def far_piece(h):
        far = piece(h, x_far)
        got(far.at[low], RING + 10 * h + 4)
        got(far.at[high], RING + 10 * h + 5)
        copy(far, far, RING + 10 * h + 9, core).start()

    relay(0)
    far_piece(0)
    relay(1)
    rows_in(ft, T_Y)

    def chunk(q):
        h, kk, c0 = lax.div(q, 4), lax.rem(lax.div(q, 2), 2), pl.multiple_of(lax.rem(q, 2) * 256, 256)
        return wb[h, kk, :, :, pl.ds(c0, 256)].reshape(384, 256), pl.ds(pl.multiple_of(q * 256, 256), 256)

    def teacher_chunk(q, carry):
        w, at = chunk(q)
        wf = w.astype(F32)
        inv = lax.rsqrt(jnp.sum(wf * wf, axis=0, keepdims=True) + EPS)
        scores = jnp.dot(ft[...].reshape(512, 384), w, preferred_element_type=F32)
        e = jnp.exp2(scores * (inv * T_SCALE))
        e_ref[:, at] = e
        col = jnp.sum(e, axis=0, keepdims=True)
        for n in range(2):
            part = slice(128 * n, 128 * n + 128)
            ivec[pl.ds(2 * q + n, 1), :] = inv[:, part]
            csum[pl.ds(2 * q + n, 1), :] = col[:, part]
        return carry

    def teacher_part(h, kk):
        lax.fori_loop(0, 2, lambda c, carry: teacher_chunk(4 * h + 2 * kk + c, carry), 0)

    for h in range(2):
        if h == 1:
            far_piece(1)
        teacher_part(h, k)
        if h == 1:
            rows_on(fs, S_Y)
        for n in range(4):
            got(piece(h, x), RING + 10 * h + 6 + n)
        teacher_part(h, 1 - k)

    def columns_start(it):
        c_send[it] = csum[...].astype(BF16)
        for i in FAR_FIRST:
            copy(c_send.at[it], c_buf.at[it, i - 1], COLS + it, xk_peer(i)).start()

    def columns_end(it):
        got(c_buf.at[it], COLS + it)
        cvec[...] = 1.0 / fold([c_send[it].astype(F32)] + [c_buf[it, i].astype(F32) for i in range(7)])

    def row_pass():
        scale = [cvec[q:q + 1, :] for q in range(16)]

        def body(i, carry):
            rows = pl.ds(pl.multiple_of(i * 16, 16), 16)
            rowacc[rows, :] = fold([e_ref[rows, 128 * q:128 * q + 128] * scale[q] for q in range(16)])
            return carry

        lax.fori_loop(0, 32, body, 0, unroll=4)

    def lanes(ref):
        return [jnp.sum(jnp.transpose(ref[128 * j:128 * j + 128, :]), axis=0, keepdims=True) for j in range(4)]

    def put(dst, at, sums):
        for j in range(4):
            dst[at + j:at + j + 1, :] = sums[j]

    def row_refs(it):
        if it == 2:
            return lry_send, lry_buf, lrz_send, lrz_buf
        return ry_send.at[it], ry_buf.at[it], rz_send.at[it], rz_buf.at[it]

    def added(own, buf):
        return fold([own[...]] + [buf[i] for i in range(7)])

    def rows_start(it):
        y_send, y_buf, _, _ = row_refs(it)
        put(y_send, 0, lanes(rowacc))
        for i in FAR_FIRST:
            copy(y_send, y_buf.at[i - 1], ROW_Y + it, y_peer(i)).start()

    def rows_middle(it):
        y_send, y_buf, z_send, z_buf = row_refs(it)
        got(y_buf, ROW_Y + it)
        z_send[...] = added(y_send, y_buf)
        for i in FAR_FIRST:
            copy(z_send, z_buf.at[i - 1], ROW_Z + it, z_peer(i)).start()

    def turn(row):
        return jnp.transpose(jnp.broadcast_to(row, (128, 128)))

    def rows_end(it):
        _, _, z_send, z_buf = row_refs(it)
        got(z_buf, ROW_Z + it)
        total = added(z_send, z_buf)
        r = 1.0 / total[0:4, :]
        for j in range(4):
            rb[128 * j:128 * j + 128, :] = turn(r[j:j + 1, :])
        return total

    def column_pass():
        def body(i, acc):
            rows = pl.ds(pl.multiple_of(i * 8, 8), 8)
            r8 = rb[rows, :]
            return tuple(acc[q] + e_ref[rows, 128 * q:128 * q + 128] * r8 for q in range(16))

        acc = lax.fori_loop(0, 64, body, tuple(jnp.zeros((8, 128), F32) for _ in range(16)), unroll=4)
        for q in range(16):
            csum[q:q + 1, :] = jnp.sum(acc[q], axis=0, keepdims=True)

    def student_chunk(q, carry):
        w, at = chunk(q)
        inv = jnp.concatenate([ivec[pl.ds(2 * q, 1), :], ivec[pl.ds(2 * q + 1, 1), :]], axis=1)
        logits = jnp.dot(fs[...].reshape(512, 384), w, preferred_element_type=F32) * (inv * S_SCALE)
        l_ref[:, at] = logits
        p = jnp.exp2(logits)
        eacc[...] += p[:, :128] + p[:, 128:]
        pb[:, at] = (p * inv).astype(BF16)
        return carry

    def product(first, last):
        total = None
        for n in range(4):
            h, kk = divmod(n, 2)
            term = lax.dot_general(
                pb[:, 512 * n:512 * n + 512], wb[h, kk].reshape(384, 512)[first:last], NT, preferred_element_type=F32
            )
            total = term if total is None else total + term
        return total

    def gradient(p, dst):
        gs[...] = product(128 * p, 128 * p + 128)
        for i in range(8):
            at = [crops(i, j) if p < 2 else crops(j, i) for j in range(8)]
            dst[p, i] = jnp.concatenate([gs[rows, :] for rows in at], axis=0).astype(BF16)

    def spread(p, src, dst, sem):
        me, peer = (a_me, a_peer) if p < 2 else (b_me, b_peer)
        for i in FAR_FIRST:
            copy(src.at[p, lax.rem(me + i, 8)], dst.at[p, i - 1], sem + p, peer(i)).start()

    def gathered(p, src, dst, sem):
        got(dst.at[p], sem + p)
        own = src[p, a_me if p < 2 else b_me]
        return fold([own.astype(F32)] + [dst[p, i].astype(F32) for i in range(7)])

    def students(first, last):
        lax.fori_loop(first, last, student_chunk, 0)

    columns_start(0)
    lry_send[...] = jnp.zeros_like(lry_send)
    eacc[...] = jnp.zeros_like(eacc)
    rows_in(fs, S_Y)
    students(0, 2)
    columns_end(0)
    row_pass()
    rows_start(0)
    students(2, 4)
    rows_middle(0)
    students(4, 6)
    rows_end(0)
    column_pass()
    columns_start(1)
    students(6, 8)
    columns_end(1)
    row_pass()
    rows_start(1)
    gradient(0, g1_send)
    rows_middle(1)
    spread(0, g1_send, g1_buf, G1)
    gradient(1, g1_send)
    rows_end(1)
    column_pass()
    columns_start(2)
    spread(1, g1_send, g1_buf, G1)
    gradient(2, g1_send)
    spread(2, g1_send, g1_buf, G1)
    loads[3].wait()
    col_cot[...] = turn(cot_ref[...])
    s16 = unit_rows(s_ref[...].astype(F32))
    s8, inv8 = (jnp.where(half == 0, v[0:8], v[8:16]) for v in s16)
    put(lry_send, 8, lanes(eacc))
    own_unit[...] = jnp.dot(s8, perm_ref[...].astype(F32), precision=HIGHEST, preferred_element_type=F32)
    columns_end(2)

    c_rows = [cvec[q:q + 1, :] for q in range(16)]
    i_rows = [ivec[q:q + 1, :] for q in range(16)]

    def last_pass(i, carry):
        rows = pl.ds(pl.multiple_of(i * 16, 16), 16)
        acc, acc2 = [], []
        for q in range(16):
            at = slice(128 * q, 128 * q + 128)
            v = e_ref[rows, at] * c_rows[q]
            acc.append(v)
            acc2.append(v * l_ref[rows, at])
            pb[rows, at] = (v * i_rows[q]).astype(BF16)
        rowacc[rows, :] = fold(acc)
        rowacc2[rows, :] = fold(acc2)
        return carry

    lax.fori_loop(0, 32, last_pass, 0, unroll=2)
    put(lry_send, 4, lanes(rowacc2))
    rows_start(2)
    gradient(0, g2_send)
    spread(0, g2_send, g2_buf, G2)
    gradient(2, g2_send)
    spread(2, g2_send, g2_buf, G2)
    rows_middle(2)
    gradient(1, g2_send)
    spread(1, g2_send, g2_buf, G2)

    def sum_blocks(own, buf):
        return fold([own.astype(F32)] + [buf[i].astype(F32) for i in range(7)])

    def wide(block, times):
        return jnp.concatenate([block] * times, axis=1)

    g1 = [gathered(p, g1_send, g1_buf, G1) for p in range(3)]
    total = rows_end(2)
    vec[...] = total
    inv_total = 1.0 / total[8:12, :]
    for j in range(4):
        xb[128 * j:128 * j + 128, :] = turn(inv_total[j:j + 1, :])
    col_x[...] = turn(vec[pl.ds(lax.div(y, 2) + 4, 1), :])
    g2b = gathered(2, g2_send, g2_buf, G2)
    for a in range(8):
        rows, part = crops(a, b_me), slice(8 * a, 8 * a + 8)
        ub_send[a] = g1[2][part] * xb[rows, :] - g2b[part] * rb[rows, :]
    for i in FAR_FIRST:
        copy(ub_send.at[lax.rem(a_me + i, 8)], ub_buf.at[i - 1], U_B, a_peer(i)).start()
    g2a = [gathered(p, g2_send, g2_buf, G2) for p in range(2)]
    for b in range(8):
        rows, part = crops(a_me, b), slice(8 * b, 8 * b + 8)
        u = [g1[p][part] * xb[rows, :] - g2a[p][part] * rb[rows, :] for p in range(2)]
        ua_send[b] = jnp.concatenate(u, axis=0).astype(BF16)
    for i in FAR_FIRST:
        copy(ua_send.at[lax.rem(b_me + i, 8)], ua_buf.at[i - 1], U_A, b_peer(i)).start()

    rows8 = pl.ds(pl.multiple_of(y * 64 + z * 8, 8), 8)
    cross = rb[rows8, :] * col_x[pl.ds(pl.multiple_of(half * 64 + z * 8, 8), 8), :]
    loss8 = -jnp.log(xb[rows8, :]) - math.log(2.0) * cross
    cot8 = wide(col_cot[pl.ds(pl.multiple_of(k * 64 + y * 8, 8), 8), :], 3)
    got(ub_buf, U_B)
    u_b = added(ub_send.at[a_me], ub_buf)
    got(ua_buf, U_A)
    u_a = sum_blocks(ua_send[b_me], ua_buf)
    u8 = jnp.concatenate([u_a[:8], u_a[8:], u_b], axis=1) * (cot8 / 0.1)
    unit8 = own_unit[...]
    along = jnp.sum(unit8 * u8, axis=1, keepdims=True)
    result = ((u8 - unit8 * along) * inv8).astype(BF16)
    result = lax.dot_general(result, perm_ref[...], NT, preferred_element_type=F32)
    first = loss8.astype(BF16).astype(F32)
    loss8 = jnp.where(lax.broadcasted_iota(jnp.int32, (8, 128), 1) < 64, first, loss8 - first)
    low_rows, high_rows = result[:, :256], jnp.concatenate([result[:, 256:], loss8], axis=1)
    result = jnp.concatenate([low_rows, high_rows], axis=0).astype(BF16)
    fin_send[...] = result
    slot = k * 8 + y
    fin_buf[slot] = result
    for i in FAR_FIRST:
        copy(fin_send, fin_buf.at[slot], FIN, y_peer(i)).start()
        copy(fin_send, fin_buf.at[slot], FIN, y_cross(i)).start()
    copy(fin_send, fin_buf.at[slot], FIN, core).start()
    got(fin_buf.at[pl.ds(0, 15)], FIN)
    out = fin_buf[...].astype(F32)
    grad_ref[:, :256] = out[:, :8, :].reshape(128, 256)
    grad_ref[:, 256:] = out[:, 8:, :128].reshape(128, 128)
    losses = jnp.transpose(out[:, 8:, 128:].reshape(128, 128))
    loss_ref[...] = losses[0:1, :] + losses[64:65, :]

    sent(fz_buf.at[pl.ds(0, 7)], F_Z)
    for buf, at in ((ft, T_Y), (fs, S_Y)):
        sent(buf.at[pl.ds(0, 2)], at)
        sent(buf.at[y], at + 1)
        sent(buf.at[y], at + 2)
        sent(buf.at[pl.ds(0, 3)], at + 3)
    for h in range(2):
        at, own = RING + 10 * h, piece(h, x)
        sent(wz_buf.at[h, pl.ds(0, 7)], W_Z + h)
        for n in range(6):
            sent(own.at[low], at + n)
        for n in range(6, 10):
            sent(own, at + n)
    for it in range(3):
        sent(c_buf.at[it], COLS + it)
        _, y_buf, _, z_buf = row_refs(it)
        sent(y_buf, ROW_Y + it)
        sent(z_buf, ROW_Z + it)
    for p in range(3):
        sent(g1_buf.at[p], G1 + p)
        sent(g2_buf.at[p], G2 + p)
    for buf, sem in (
        (ua_buf, U_A), (ub_buf, U_B),
        (fin_buf.at[pl.ds(0, 15)], FIN),
    ):
        sent(buf, sem)


def shards(teacher, student, proto_weight, cotangent):
    vmem, hbm = pl.BlockSpec(memory_space=pltpu.VMEM), pl.BlockSpec(memory_space=pltpu.HBM)
    v = pltpu.VMEM
    operands = (teacher, student, proto_weight, cotangent.reshape(1, 128))
    grad, loss = pl.pallas_call(
        kernel,
        out_shape=(v((128, 384), F32), v((1, 128), F32)),
        in_specs=[hbm] * 4,
        out_specs=(vmem, vmem),
        scratch_shapes=[
            v((16, 384), BF16), v((16, 384), BF16), v((12, 8192), BF16), v((1, 128), F32), v((384, 384), BF16),
            v((768, 128), F32), v((2, 8, 48, 128), BF16), v((2, 8, 48, 128), BF16), v((8, 48, 128), F32),
            v((96, 512), F32), v((2, 2, 4, 96, 512), BF16),
            v((48, 128), BF16), v((8, 48, 128), BF16), v((8, 64, 384), BF16), v((8, 64, 384), BF16),
            v((512, 2048), F32), v((512, 2048), F32), v((512, 2048), BF16),
            v((512, 128), F32), v((512, 128), F32), v((512, 128), F32), v((512, 128), F32), v((512, 128), F32),
            v((16, 128), F32), v((16, 128), F32),
            v((3, 16, 128), BF16), v((3, 7, 16, 128), BF16),
            v((2, 4, 128), F32), v((2, 7, 4, 128), F32), v((2, 4, 128), F32), v((2, 7, 4, 128), F32),
            v((512, 128), F32),
            v((3, 8, 64, 128), BF16), v((3, 7, 64, 128), BF16), v((3, 8, 64, 128), BF16), v((3, 7, 64, 128), BF16),
            v((8, 16, 128), BF16), v((7, 16, 128), BF16), v((8, 8, 128), F32), v((7, 8, 128), F32),
            v((16, 128), F32), v((16, 128), F32), v((16, 128), F32), v((7, 16, 128), F32), v((16, 128), F32), v((7, 16, 128), F32),
            v((128, 128), F32), v((128, 128), F32), v((8, 384), F32),
            v((16, 256), BF16), v((16, 16, 256), BF16),
            pltpu.SemaphoreType.DMA((4,)), pltpu.SemaphoreType.DMA((COUNT,)), pltpu.SemaphoreType.DMA((COUNT,)),
        ],
        compiler_params=pltpu.CompilerParams(
            collective_id=0, has_side_effects=True, vmem_limit_bytes=60 * 1024 * 1024
        ),
        cost_estimate=pl.CostEstimate(flops=2_400_000_000, bytes_accessed=4_000_000, transcendentals=2_000_000),
    )(*(pltpu.with_memory_space_constraint(a, pltpu.HBM) for a in operands))
    return loss.reshape(128), grad


def solution(mesh):
    return jax.shard_map(
        shards,
        mesh=mesh,
        in_specs=(P("dp", None), P("dp", None), P("dp", "proto"), P("dp")),
        out_specs=(P("dp"), P("dp", None)),
        check_vma=False,
    )
```

```python
import math

import jax
import jax.numpy as jnp
from jax import lax
from jax.experimental import pallas as pl
from jax.experimental.pallas import tpu as pltpu
from jax.sharding import PartitionSpec as P

EPS = 1e-06
LOG2E = math.log2(math.e)
T_SCALE = LOG2E / 0.04
S_SCALE = LOG2E / 0.1
F32, BF16 = jnp.float32, jnp.bfloat16
MESH = pl.DeviceIdType.MESH
HIGHEST = lax.Precision.HIGHEST
NT = (((1,), (1,)), ((), ()))

FAR_FIRST = (4, 3, 5, 2, 6, 1, 7)

F_Z, W_Z = 0, 1
RING = 4
COLS = 24
ROWS, LAST_Y, LAST_Z = 27, 29, 30
G1, G2 = 33, 36
U_A, U_B, FIN = 39, 40, 41
T_Y, S_Y = 42, 46
COUNT = 50


def unit_rows(values):
    inv = lax.rsqrt(jnp.sum(values * values, axis=1, keepdims=True) + EPS)
    return values * inv, inv


def fold(terms):
    while len(terms) > 1:
        terms = [a + b for a, b in zip(terms[::2], terms[1::2])]
    return terms[0]


def kernel(
    t_hbm, s_hbm, w_hbm, cot_hbm,
    grad_ref, loss_ref,
    t_ref, s_ref, w_ref, cot_ref, perm_ref,
    pack, wz_send, wz_buf, wz_wide, asm, wb,
    fz_send, fz_buf, ft, fs,
    e_ref, l_ref, pb, rowacc, rowacc2, eacc, rb, xb, ivec, cvec,
    c_send, c_buf, r_send, r_buf,
    gs, g1_send, g1_buf, g2_send, g2_buf,
    ua_send, ua_buf, ub_send, ub_buf, csum, vec, lry_send, lry_buf, lrz_send, lrz_buf,
    col_cot, col_x, own_unit,
    fin_send, fin_buf,
    lsem, ssem, rsem,
):
    dp, pr = lax.axis_index("dp"), lax.axis_index("proto")
    z, x = lax.div(dp, 4), lax.rem(dp, 4)
    y, k = lax.div(pr, 2), lax.rem(pr, 2)

    def z_peer(i):
        return (lax.rem(z + i, 8) * 4 + x, pr)

    def y_peer(i):
        return (dp, lax.rem(y + i, 8) * 2 + k)

    def xk_peer(i):
        g = lax.rem(x * 2 + k + i, 8)
        return (z * 4 + lax.div(g, 2), y * 2 + lax.rem(g, 2))

    def plane_peer(i, j):
        return (z_peer(i)[0], y_peer(j)[1])

    plane = [(i, j) for i in FAR_FIRST + (0,) for j in FAR_FIRST + (0,)][:-1]

    def y_cross(i):
        return (dp, lax.rem(y + i, 8) * 2 + 1 - k)

    def a_peer(i):
        y_at, z_at = y_peer(i)[1], z_peer(i)[0]
        return (dp + k * (z_at - dp), y_at + k * (pr - y_at))

    def b_peer(i):
        y_at, z_at = y_peer(i)[1], z_peer(i)[0]
        return (z_at + k * (dp - z_at), pr + k * (y_at - pr))

    a_me, b_me = y + k * (z - y), z + k * (y - z)
    a_step, b_step = 64 - 56 * k, 8 + 56 * k

    def crops(a, b):
        return pl.ds(pl.multiple_of(a * a_step + b * b_step, 8), 8)

    def copy(src, dst, sem, peer):
        return pltpu.make_async_remote_copy(
            src_ref=src, dst_ref=dst, send_sem=ssem.at[sem], recv_sem=rsem.at[sem],
            device_id=peer, device_id_type=MESH,
        )

    def got(ref, sem):
        copy(ref, ref, sem, (dp, pr)).wait_recv()

    def sent(ref, sem):
        copy(ref, ref, sem, (dp, pr)).wait_send()

    half = lax.rem(y, 2)
    at16 = pl.multiple_of(k * 64 + lax.div(y, 2) * 16, 16)
    rows16 = pl.ds(at16, 16)
    loads = [
        pltpu.make_async_copy(src, dst, lsem.at[n])
        for n, (src, dst) in enumerate((
            (w_hbm, w_ref), (t_hbm.at[rows16], t_ref), (s_hbm.at[rows16], s_ref), (cot_hbm, cot_ref)
        ))
    ]
    for load in loads:
        load.start()

    barrier = pltpu.get_barrier_semaphore()
    for i in range(1, 8):
        for peer in (xk_peer(i), y_cross(i)):
            pl.semaphore_signal(barrier, inc=1, device_id=peer, device_id_type=MESH)
    for i, j in plane:
        pl.semaphore_signal(barrier, inc=1, device_id=plane_peer(i, j), device_id_type=MESH)

    feature = lax.broadcasted_iota(jnp.int32, (384, 128), 0)
    fz = lax.shift_right_logical(feature * 1366, 16)
    fx = lax.shift_right_logical((feature - fz * 48) * 5462, 16)
    place = fx * 96 + fz * 12 + (feature - fz * 48 - fx * 12)
    lane = lax.broadcasted_iota(jnp.int32, (384, 128), 1)
    for n in range(3):
        perm_ref[:, 128 * n:128 * n + 128] = (place == lane + 128 * n).astype(F32).astype(BF16)

    loads[0].wait()
    for d in range(8):
        for h in range(2):
            for r in range(4):
                q, at = d * 8 + h * 4 + r, ((h * 8 + d) * 4 + r) * 12
                pack[at:at + 12, :] = w_ref[:, 128 * q:128 * q + 128].astype(F32)
    for h in range(2):
        for d in range(8):
            at = (h * 8 + d) * 48
            wz_send[h, d] = pack[at:at + 48, :].astype(BF16)
        wz_buf[h, z] = wz_send[h, z]

    pl.semaphore_wait(barrier, 77)

    def weights_out(h):
        for i in FAR_FIRST:
            copy(wz_send.at[h, lax.rem(z + i, 8)], wz_buf.at[h, z], W_Z + h, z_peer(i)).start()

    weights_out(0)
    loads[1].wait()
    loads[2].wait()
    v = jnp.concatenate([t_ref[...].astype(F32), s_ref[...].astype(F32)], axis=0)
    v = jnp.dot(unit_rows(v)[0].astype(BF16), perm_ref[...], preferred_element_type=F32)
    v = [jnp.where(half == 0, v[at:at + 8], v[at + 8:at + 16]) for at in (0, 16)]
    v = jnp.concatenate([m[:, 128 * n:128 * n + 128] for m in v for n in range(3)], axis=0).astype(BF16)
    fz_send[...] = v
    fz_buf[z] = v
    for i in FAR_FIRST:
        copy(fz_send, fz_buf.at[z], F_Z, z_peer(i)).start()
    weights_out(1)

    first, second = pl.ds(0, 32), pl.ds(32, 32)

    def rows_out(buf, at):
        block = buf.at[y]
        copy(block, block, at + 1, y_peer(2)).start()
        copy(block, block, at + 2, y_peer(6)).start()
        copy(block, block, at, y_peer(1)).start()
        copy(block, block, at, y_peer(7)).start()

    def rows_on(buf, at):
        below, above = buf.at[lax.rem(y + 6, 8)], buf.at[lax.rem(y + 2, 8)]
        got(below, at + 1)
        copy(below.at[first], below.at[first], at + 3, y_peer(2)).start()
        copy(below, below, at + 3, y_peer(1)).start()
        got(above, at + 2)
        copy(above.at[second], above.at[second], at + 3, y_peer(6)).start()
        copy(above, above, at + 3, y_peer(7)).start()

    def rows_in(buf, at):
        got(buf.at[pl.ds(0, 2)], at)
        got(buf.at[pl.ds(0, 3)], at + 3)

    x_right, x_left, x_far = lax.rem(x + 1, 4), lax.rem(x + 3, 4), lax.rem(x + 2, 4)
    right, left, core = (z * 4 + x_right, pr), (z * 4 + x_left, pr), (dp, y * 2 + 1 - k)
    low, high = pl.ds(0, 48), pl.ds(48, 48)

    def piece(h, at):
        return wb.at[h, k, at]

    for h in range(2):
        got(wz_buf.at[h, pl.ds(0, 7)], W_Z + h)
        for s in range(8):
            wz_wide[s] = wz_buf[h, s].astype(F32)
            for q in range(4):
                asm[12 * s:12 * s + 12, 128 * q:128 * q + 128] = wz_wide[s, 12 * q:12 * q + 12, :]
        wb[h, k, x] = asm[...].astype(BF16)
        own = piece(h, x)
        at = RING + 10 * h
        copy(own.at[low], own.at[low], at, right).start()
        copy(own.at[high], own.at[high], at + 2, left).start()
        copy(own.at[high], own.at[high], at + 1, right).start()
        copy(own.at[low], own.at[low], at + 3, left).start()
        copy(own, own, at + 6, core).start()
        if h == 0:
            got(fz_buf.at[pl.ds(0, 7)], F_Z)
            for buf, at in ((ft, 0), (fs, 24)):
                v = [fz_buf[d, :, :].astype(F32) for d in range(8)]
                v = [jnp.concatenate([m[at + 8 * n:at + 8 * n + 8] for m in v], axis=0) for n in range(3)]
                buf[y] = jnp.concatenate(v, axis=1).astype(BF16)
            rows_out(ft, T_Y)
        else:
            rows_on(ft, T_Y)
            rows_out(fs, S_Y)

    def relay(h):
        at, from_left, from_right = RING + 10 * h, piece(h, x_left), piece(h, x_right)
        got(from_left.at[low], at)
        copy(from_left.at[low], from_left.at[low], at + 4, right).start()
        got(from_right.at[high], at + 2)
        copy(from_right.at[high], from_right.at[high], at + 5, left).start()
        got(from_left.at[high], at + 1)
        copy(from_left, from_left, at + 7, core).start()
        got(from_right.at[low], at + 3)
        copy(from_right, from_right, at + 8, core).start()

    def far_piece(h):
        far = piece(h, x_far)
        got(far.at[low], RING + 10 * h + 4)
        got(far.at[high], RING + 10 * h + 5)
        copy(far, far, RING + 10 * h + 9, core).start()

    relay(0)
    far_piece(0)
    relay(1)
    rows_in(ft, T_Y)

    def chunk(q):
        h, kk, c0 = lax.div(q, 4), lax.rem(lax.div(q, 2), 2), pl.multiple_of(lax.rem(q, 2) * 256, 256)
        return wb[h, kk, :, :, pl.ds(c0, 256)].reshape(384, 256), pl.ds(pl.multiple_of(q * 256, 256), 256)

    def teacher_chunk(q, carry):
        w, at = chunk(q)
        wf = w.astype(F32)
        inv = lax.rsqrt(jnp.sum(wf * wf, axis=0, keepdims=True) + EPS)
        scores = jnp.dot(ft[...].reshape(512, 384), w, preferred_element_type=F32)
        e = jnp.exp2(scores * (inv * T_SCALE))
        e_ref[:, at] = e
        col = jnp.sum(e, axis=0, keepdims=True)
        for n in range(2):
            part = slice(128 * n, 128 * n + 128)
            ivec[pl.ds(2 * q + n, 1), :] = inv[:, part]
            csum[pl.ds(2 * q + n, 1), :] = col[:, part]
        return carry

    def teacher_part(h, kk):
        lax.fori_loop(0, 2, lambda c, carry: teacher_chunk(4 * h + 2 * kk + c, carry), 0)

    for h in range(2):
        if h == 1:
            far_piece(1)
        teacher_part(h, k)
        if h == 1:
            rows_on(fs, S_Y)
        for n in range(4):
            got(piece(h, x), RING + 10 * h + 6 + n)
        teacher_part(h, 1 - k)

    def columns_start(it):
        c_send[it] = csum[...].astype(BF16)
        for i in FAR_FIRST:
            copy(c_send.at[it], c_buf.at[it, i - 1], COLS + it, xk_peer(i)).start()

    def columns_end(it):
        got(c_buf.at[it], COLS + it)
        cvec[...] = 1.0 / fold([c_send[it].astype(F32)] + [c_buf[it, i].astype(F32) for i in range(7)])

    def row_pass():
        scale = [cvec[q:q + 1, :] for q in range(16)]

        def body(i, carry):
            rows = pl.ds(pl.multiple_of(i * 16, 16), 16)
            rowacc[rows, :] = fold([e_ref[rows, 128 * q:128 * q + 128] * scale[q] for q in range(16)])
            return carry

        lax.fori_loop(0, 32, body, 0, unroll=4)

    def lanes(ref):
        return [jnp.sum(jnp.transpose(ref[128 * j:128 * j + 128, :]), axis=0, keepdims=True) for j in range(4)]

    def put(dst, at, sums):
        for j in range(4):
            dst[at + j:at + j + 1, :] = sums[j]

    def tree(terms):
        while len(terms) > 1:
            pairs = [a + b for a, b in zip(terms[::2], terms[1::2])]
            terms = pairs + terms[2 * len(pairs):]
        return terms[0]

    def added(own, buf):
        return tree([own[...]] + [buf[i] for i in range(buf.shape[0])])

    def turn(row):
        return jnp.transpose(jnp.broadcast_to(row, (128, 128)))

    def set_row_scale(total):
        r = 1.0 / total[0:4, :]
        for j in range(4):
            rb[128 * j:128 * j + 128, :] = turn(r[j:j + 1, :])

    def rows_start(it):
        put(r_send.at[it], 0, lanes(rowacc))
        for n, (i, j) in enumerate(plane):
            copy(r_send.at[it], r_buf.at[it, n], ROWS + it, plane_peer(i, j)).start()

    def rows_end(it):
        got(r_buf.at[it], ROWS + it)
        set_row_scale(added(r_send.at[it], r_buf.at[it]))

    def last_rows_start():
        put(lry_send, 0, lanes(rowacc))
        for i in FAR_FIRST:
            copy(lry_send, lry_buf.at[i - 1], LAST_Y, y_peer(i)).start()

    def last_rows_middle():
        got(lry_buf, LAST_Y)
        lrz_send[...] = added(lry_send, lry_buf)
        for i in FAR_FIRST:
            copy(lrz_send, lrz_buf.at[i - 1], LAST_Z, z_peer(i)).start()

    def last_rows_end():
        got(lrz_buf, LAST_Z)
        total = added(lrz_send, lrz_buf)
        set_row_scale(total)
        return total

    def column_pass():
        def body(i, acc):
            rows = pl.ds(pl.multiple_of(i * 8, 8), 8)
            r8 = rb[rows, :]
            return tuple(acc[q] + e_ref[rows, 128 * q:128 * q + 128] * r8 for q in range(16))

        acc = lax.fori_loop(0, 64, body, tuple(jnp.zeros((8, 128), F32) for _ in range(16)), unroll=4)
        for q in range(16):
            csum[q:q + 1, :] = jnp.sum(acc[q], axis=0, keepdims=True)

    def student_chunk(q, carry):
        w, at = chunk(q)
        inv = jnp.concatenate([ivec[pl.ds(2 * q, 1), :], ivec[pl.ds(2 * q + 1, 1), :]], axis=1)
        logits = jnp.dot(fs[...].reshape(512, 384), w, preferred_element_type=F32) * (inv * S_SCALE)
        l_ref[:, at] = logits
        p = jnp.exp2(logits)
        eacc[...] += p[:, :128] + p[:, 128:]
        pb[:, at] = (p * inv).astype(BF16)
        return carry

    def product(first, last):
        total = None
        for n in range(4):
            h, kk = divmod(n, 2)
            term = lax.dot_general(
                pb[:, 512 * n:512 * n + 512], wb[h, kk].reshape(384, 512)[first:last], NT, preferred_element_type=F32
            )
            total = term if total is None else total + term
        return total

    def gradient(p, dst):
        gs[...] = product(128 * p, 128 * p + 128)
        for i in range(8):
            at = [crops(i, j) if p < 2 else crops(j, i) for j in range(8)]
            dst[p, i] = jnp.concatenate([gs[rows, :] for rows in at], axis=0).astype(BF16)

    def spread(p, src, dst, sem):
        me, peer = (a_me, a_peer) if p < 2 else (b_me, b_peer)
        for i in FAR_FIRST:
            copy(src.at[p, lax.rem(me + i, 8)], dst.at[p, i - 1], sem + p, peer(i)).start()

    def gathered(p, src, dst, sem):
        got(dst.at[p], sem + p)
        own = src[p, a_me if p < 2 else b_me]
        return fold([own.astype(F32)] + [dst[p, i].astype(F32) for i in range(7)])

    def students(first, last):
        lax.fori_loop(first, last, student_chunk, 0)

    columns_start(0)
    lry_send[...] = jnp.zeros_like(lry_send)
    eacc[...] = jnp.zeros_like(eacc)
    rows_in(fs, S_Y)
    students(0, 2)
    columns_end(0)
    row_pass()
    rows_start(0)
    students(2, 5)
    rows_end(0)
    column_pass()
    columns_start(1)
    students(5, 8)
    columns_end(1)
    row_pass()
    rows_start(1)
    gradient(0, g1_send)
    gradient(1, g1_send)
    rows_end(1)
    spread(0, g1_send, g1_buf, G1)
    column_pass()
    columns_start(2)
    spread(1, g1_send, g1_buf, G1)
    gradient(2, g1_send)
    spread(2, g1_send, g1_buf, G1)
    loads[3].wait()
    col_cot[...] = turn(cot_ref[...])
    s16 = unit_rows(s_ref[...].astype(F32))
    s8, inv8 = (jnp.where(half == 0, v[0:8], v[8:16]) for v in s16)
    put(lry_send, 8, lanes(eacc))
    own_unit[...] = jnp.dot(s8, perm_ref[...].astype(F32), precision=HIGHEST, preferred_element_type=F32)
    columns_end(2)

    c_rows = [cvec[q:q + 1, :] for q in range(16)]
    i_rows = [ivec[q:q + 1, :] for q in range(16)]

    def last_pass(i, carry):
        rows = pl.ds(pl.multiple_of(i * 16, 16), 16)
        acc, acc2 = [], []
        for q in range(16):
            at = slice(128 * q, 128 * q + 128)
            v = e_ref[rows, at] * c_rows[q]
            acc.append(v)
            acc2.append(v * l_ref[rows, at])
            pb[rows, at] = (v * i_rows[q]).astype(BF16)
        rowacc[rows, :] = fold(acc)
        rowacc2[rows, :] = fold(acc2)
        return carry

    lax.fori_loop(0, 32, last_pass, 0, unroll=2)
    put(lry_send, 4, lanes(rowacc2))
    last_rows_start()
    gradient(0, g2_send)
    spread(0, g2_send, g2_buf, G2)
    gradient(2, g2_send)
    spread(2, g2_send, g2_buf, G2)
    last_rows_middle()
    gradient(1, g2_send)
    spread(1, g2_send, g2_buf, G2)

    def sum_blocks(own, buf):
        return fold([own.astype(F32)] + [buf[i].astype(F32) for i in range(7)])

    def wide(block, times):
        return jnp.concatenate([block] * times, axis=1)

    g1 = [gathered(p, g1_send, g1_buf, G1) for p in range(3)]
    total = last_rows_end()
    vec[...] = total
    inv_total = 1.0 / total[8:12, :]
    for j in range(4):
        xb[128 * j:128 * j + 128, :] = turn(inv_total[j:j + 1, :])
    col_x[...] = turn(vec[pl.ds(lax.div(y, 2) + 4, 1), :])
    g2b = gathered(2, g2_send, g2_buf, G2)
    for a in range(8):
        rows, part = crops(a, b_me), slice(8 * a, 8 * a + 8)
        ub_send[a] = g1[2][part] * xb[rows, :] - g2b[part] * rb[rows, :]
    for i in FAR_FIRST:
        copy(ub_send.at[lax.rem(a_me + i, 8)], ub_buf.at[i - 1], U_B, a_peer(i)).start()
    g2a = [gathered(p, g2_send, g2_buf, G2) for p in range(2)]
    for b in range(8):
        rows, part = crops(a_me, b), slice(8 * b, 8 * b + 8)
        u = [g1[p][part] * xb[rows, :] - g2a[p][part] * rb[rows, :] for p in range(2)]
        ua_send[b] = jnp.concatenate(u, axis=0).astype(BF16)
    for i in FAR_FIRST:
        copy(ua_send.at[lax.rem(b_me + i, 8)], ua_buf.at[i - 1], U_A, b_peer(i)).start()

    rows8 = pl.ds(pl.multiple_of(y * 64 + z * 8, 8), 8)
    cross = rb[rows8, :] * col_x[pl.ds(pl.multiple_of(half * 64 + z * 8, 8), 8), :]
    loss8 = -jnp.log(xb[rows8, :]) - math.log(2.0) * cross
    cot8 = wide(col_cot[pl.ds(pl.multiple_of(k * 64 + y * 8, 8), 8), :], 3)
    got(ub_buf, U_B)
    u_b = added(ub_send.at[a_me], ub_buf)
    got(ua_buf, U_A)
    u_a = sum_blocks(ua_send[b_me], ua_buf)
    u8 = jnp.concatenate([u_a[:8], u_a[8:], u_b], axis=1) * (cot8 / 0.1)
    unit8 = own_unit[...]
    along = jnp.sum(unit8 * u8, axis=1, keepdims=True)
    result = ((u8 - unit8 * along) * inv8).astype(BF16)
    result = lax.dot_general(result, perm_ref[...], NT, preferred_element_type=F32)
    first = loss8.astype(BF16).astype(F32)
    loss8 = jnp.where(lax.broadcasted_iota(jnp.int32, (8, 128), 1) < 64, first, loss8 - first)
    low_rows, high_rows = result[:, :256], jnp.concatenate([result[:, 256:], loss8], axis=1)
    result = jnp.concatenate([low_rows, high_rows], axis=0).astype(BF16)
    fin_send[...] = result
    slot = k * 8 + y
    fin_buf[slot] = result
    for i in FAR_FIRST:
        copy(fin_send, fin_buf.at[slot], FIN, y_peer(i)).start()
        copy(fin_send, fin_buf.at[slot], FIN, y_cross(i)).start()
    copy(fin_send, fin_buf.at[slot], FIN, core).start()
    got(fin_buf.at[pl.ds(0, 15)], FIN)
    out = fin_buf[...].astype(F32)
    grad_ref[:, :256] = out[:, :8, :].reshape(128, 256)
    grad_ref[:, 256:] = out[:, 8:, :128].reshape(128, 128)
    losses = jnp.transpose(out[:, 8:, 128:].reshape(128, 128))
    loss_ref[...] = losses[0:1, :] + losses[64:65, :]

    sent(fz_buf.at[pl.ds(0, 7)], F_Z)
    for buf, at in ((ft, T_Y), (fs, S_Y)):
        sent(buf.at[pl.ds(0, 2)], at)
        sent(buf.at[y], at + 1)
        sent(buf.at[y], at + 2)
        sent(buf.at[pl.ds(0, 3)], at + 3)
    for h in range(2):
        at, own = RING + 10 * h, piece(h, x)
        sent(wz_buf.at[h, pl.ds(0, 7)], W_Z + h)
        for n in range(6):
            sent(own.at[low], at + n)
        for n in range(6, 10):
            sent(own, at + n)
    for it in range(3):
        sent(c_buf.at[it], COLS + it)
    for it in range(2):
        sent(r_buf.at[it], ROWS + it)
    sent(lry_buf, LAST_Y)
    sent(lrz_buf, LAST_Z)
    for p in range(3):
        sent(g1_buf.at[p], G1 + p)
        sent(g2_buf.at[p], G2 + p)
    for buf, sem in (
        (ua_buf, U_A), (ub_buf, U_B),
        (fin_buf.at[pl.ds(0, 15)], FIN),
    ):
        sent(buf, sem)


def shards(teacher, student, proto_weight, cotangent):
    vmem, hbm = pl.BlockSpec(memory_space=pltpu.VMEM), pl.BlockSpec(memory_space=pltpu.HBM)
    v = pltpu.VMEM
    operands = (teacher, student, proto_weight, cotangent.reshape(1, 128))
    grad, loss = pl.pallas_call(
        kernel,
        out_shape=(v((128, 384), F32), v((1, 128), F32)),
        in_specs=[hbm] * 4,
        out_specs=(vmem, vmem),
        scratch_shapes=[
            v((16, 384), BF16), v((16, 384), BF16), v((12, 8192), BF16), v((1, 128), F32), v((384, 384), BF16),
            v((768, 128), F32), v((2, 8, 48, 128), BF16), v((2, 8, 48, 128), BF16), v((8, 48, 128), F32),
            v((96, 512), F32), v((2, 2, 4, 96, 512), BF16),
            v((48, 128), BF16), v((8, 48, 128), BF16), v((8, 64, 384), BF16), v((8, 64, 384), BF16),
            v((512, 2048), F32), v((512, 2048), F32), v((512, 2048), BF16),
            v((512, 128), F32), v((512, 128), F32), v((512, 128), F32), v((512, 128), F32), v((512, 128), F32),
            v((16, 128), F32), v((16, 128), F32),
            v((3, 16, 128), BF16), v((3, 7, 16, 128), BF16),
            v((2, 4, 128), F32), v((2, 63, 4, 128), F32),
            v((512, 128), F32),
            v((3, 8, 64, 128), BF16), v((3, 7, 64, 128), BF16), v((3, 8, 64, 128), BF16), v((3, 7, 64, 128), BF16),
            v((8, 16, 128), BF16), v((7, 16, 128), BF16), v((8, 8, 128), F32), v((7, 8, 128), F32),
            v((16, 128), F32), v((16, 128), F32), v((16, 128), F32), v((7, 16, 128), F32), v((16, 128), F32), v((7, 16, 128), F32),
            v((128, 128), F32), v((128, 128), F32), v((8, 384), F32),
            v((16, 256), BF16), v((16, 16, 256), BF16),
            pltpu.SemaphoreType.DMA((4,)), pltpu.SemaphoreType.DMA((COUNT,)), pltpu.SemaphoreType.DMA((COUNT,)),
        ],
        compiler_params=pltpu.CompilerParams(
            collective_id=0, has_side_effects=True, vmem_limit_bytes=60 * 1024 * 1024
        ),
        cost_estimate=pl.CostEstimate(flops=2_400_000_000, bytes_accessed=4_000_000, transcendentals=2_000_000),
    )(*(pltpu.with_memory_space_constraint(a, pltpu.HBM) for a in operands))
    return loss.reshape(128), grad


def solution(mesh):
    return jax.shard_map(
        shards,
        mesh=mesh,
        in_specs=(P("dp", None), P("dp", None), P("dp", "proto"), P("dp")),
        out_specs=(P("dp"), P("dp", None)),
        check_vma=False,
    )
```

```python
import math

import jax
import jax.numpy as jnp
from jax import lax
from jax.experimental import pallas as pl
from jax.experimental.pallas import tpu as pltpu
from jax.sharding import PartitionSpec as P

EPS = 1e-06
LOG2E = math.log2(math.e)
T_SCALE = LOG2E / 0.04
S_SCALE = LOG2E / 0.1
F32, BF16 = jnp.float32, jnp.bfloat16
MESH = pl.DeviceIdType.MESH
HIGHEST = lax.Precision.HIGHEST
NT = (((1,), (1,)), ((), ()))

FAR_FIRST = (4, 3, 5, 2, 6, 1, 7)

F_Z, W_Z = 0, 1
RING = 4
COLS = 24
ROWS, LAST_Y, LAST_Z = 27, 29, 30
G1, G2 = 33, 36
U_A, U_B, FIN = 39, 40, 41
T_Y, S_Y = 42, 46
COUNT = 50


def unit_rows(values):
    inv = lax.rsqrt(jnp.sum(values * values, axis=1, keepdims=True) + EPS)
    return values * inv, inv


def fold(terms):
    while len(terms) > 1:
        terms = [a + b for a, b in zip(terms[::2], terms[1::2])]
    return terms[0]


def kernel(
    t_hbm, s_hbm, w_hbm, cot_hbm,
    grad_ref, loss_ref,
    t_ref, s_ref, w_ref, cot_ref, perm_ref,
    pack, wz_send, wz_buf, wz_wide, asm, wb,
    fz_send, fz_buf, ft, fs,
    e_ref, l_ref, pb, rowacc, rowacc2, eacc, rb, xb, ivec, cvec,
    c_send, c_buf, r_send, r_buf,
    gs, g1_send, g1_buf, g2_send, g2_buf,
    ua_send, ua_buf, ub_send, ub_buf, csum, vec, lry_send, lry_buf, lrz_send, lrz_buf,
    col_cot, col_x, own_unit,
    fin_send, fin_buf,
    lsem, ssem, rsem,
):
    dp, pr = lax.axis_index("dp"), lax.axis_index("proto")
    z, x = lax.div(dp, 4), lax.rem(dp, 4)
    y, k = lax.div(pr, 2), lax.rem(pr, 2)

    def z_peer(i):
        return (lax.rem(z + i, 8) * 4 + x, pr)

    def y_peer(i):
        return (dp, lax.rem(y + i, 8) * 2 + k)

    def xk_peer(i):
        g = lax.rem(x * 2 + k + i, 8)
        return (z * 4 + lax.div(g, 2), y * 2 + lax.rem(g, 2))

    def plane_peer(i, j):
        return (z_peer(i)[0], y_peer(j)[1])

    plane = [(i, j) for i in FAR_FIRST + (0,) for j in FAR_FIRST + (0,)][:-1]

    def y_cross(i):
        return (dp, lax.rem(y + i, 8) * 2 + 1 - k)

    def a_peer(i):
        y_at, z_at = y_peer(i)[1], z_peer(i)[0]
        return (dp + k * (z_at - dp), y_at + k * (pr - y_at))

    def b_peer(i):
        y_at, z_at = y_peer(i)[1], z_peer(i)[0]
        return (z_at + k * (dp - z_at), pr + k * (y_at - pr))

    a_me, b_me = y + k * (z - y), z + k * (y - z)
    a_step, b_step = 64 - 56 * k, 8 + 56 * k

    def crops(a, b):
        return pl.ds(pl.multiple_of(a * a_step + b * b_step, 8), 8)

    def copy(src, dst, sem, peer):
        return pltpu.make_async_remote_copy(
            src_ref=src, dst_ref=dst, send_sem=ssem.at[sem], recv_sem=rsem.at[sem],
            device_id=peer, device_id_type=MESH,
        )

    def got(ref, sem):
        copy(ref, ref, sem, (dp, pr)).wait_recv()

    def sent(ref, sem):
        copy(ref, ref, sem, (dp, pr)).wait_send()

    half = lax.rem(y, 2)
    at16 = pl.multiple_of(k * 64 + lax.div(y, 2) * 16, 16)
    rows16 = pl.ds(at16, 16)
    loads = [
        pltpu.make_async_copy(src, dst, lsem.at[n])
        for n, (src, dst) in enumerate((
            (w_hbm, w_ref), (t_hbm.at[rows16], t_ref), (s_hbm.at[rows16], s_ref), (cot_hbm, cot_ref)
        ))
    ]
    for load in loads:
        load.start()

    barrier = pltpu.get_barrier_semaphore()
    for i in range(1, 8):
        for peer in (xk_peer(i), y_cross(i)):
            pl.semaphore_signal(barrier, inc=1, device_id=peer, device_id_type=MESH)
    for i, j in plane:
        pl.semaphore_signal(barrier, inc=1, device_id=plane_peer(i, j), device_id_type=MESH)

    feature = lax.broadcasted_iota(jnp.int32, (384, 128), 0)
    fz = lax.shift_right_logical(feature * 1366, 16)
    fx = lax.shift_right_logical((feature - fz * 48) * 5462, 16)
    place = fx * 96 + fz * 12 + (feature - fz * 48 - fx * 12)
    lane = lax.broadcasted_iota(jnp.int32, (384, 128), 1)
    for n in range(3):
        perm_ref[:, 128 * n:128 * n + 128] = (place == lane + 128 * n).astype(F32).astype(BF16)

    loads[0].wait()
    for d in range(8):
        for h in range(2):
            for r in range(4):
                q, at = d * 8 + h * 4 + r, ((h * 8 + d) * 4 + r) * 12
                pack[at:at + 12, :] = w_ref[:, 128 * q:128 * q + 128].astype(F32)
    for h in range(2):
        for d in range(8):
            at = (h * 8 + d) * 48
            wz_send[h, d] = pack[at:at + 48, :].astype(BF16)
        wz_buf[h, z] = wz_send[h, z]

    pl.semaphore_wait(barrier, 77)

    def weights_out(h):
        for i in FAR_FIRST:
            copy(wz_send.at[h, lax.rem(z + i, 8)], wz_buf.at[h, z], W_Z + h, z_peer(i)).start()

    weights_out(0)
    loads[1].wait()
    loads[2].wait()
    v = jnp.concatenate([t_ref[...].astype(F32), s_ref[...].astype(F32)], axis=0)
    v = jnp.dot(unit_rows(v)[0].astype(BF16), perm_ref[...], preferred_element_type=F32)
    v = [jnp.where(half == 0, v[at:at + 8], v[at + 8:at + 16]) for at in (0, 16)]
    v = jnp.concatenate([m[:, 128 * n:128 * n + 128] for m in v for n in range(3)], axis=0).astype(BF16)
    fz_send[...] = v
    fz_buf[z] = v
    for i in FAR_FIRST:
        copy(fz_send, fz_buf.at[z], F_Z, z_peer(i)).start()
    weights_out(1)

    first, second = pl.ds(0, 32), pl.ds(32, 32)

    def rows_out(buf, at):
        block = buf.at[y]
        copy(block, block, at + 1, y_peer(2)).start()
        copy(block, block, at + 2, y_peer(6)).start()
        copy(block, block, at, y_peer(1)).start()
        copy(block, block, at, y_peer(7)).start()

    def rows_on(buf, at):
        below, above = buf.at[lax.rem(y + 6, 8)], buf.at[lax.rem(y + 2, 8)]
        got(below, at + 1)
        copy(below.at[first], below.at[first], at + 3, y_peer(2)).start()
        copy(below, below, at + 3, y_peer(1)).start()
        got(above, at + 2)
        copy(above.at[second], above.at[second], at + 3, y_peer(6)).start()
        copy(above, above, at + 3, y_peer(7)).start()

    def rows_in(buf, at):
        got(buf.at[pl.ds(0, 2)], at)
        got(buf.at[pl.ds(0, 3)], at + 3)

    x_right, x_left, x_far = lax.rem(x + 1, 4), lax.rem(x + 3, 4), lax.rem(x + 2, 4)
    right, left, core = (z * 4 + x_right, pr), (z * 4 + x_left, pr), (dp, y * 2 + 1 - k)
    low, high = pl.ds(0, 48), pl.ds(48, 48)

    def piece(h, at):
        return wb.at[h, k, at]

    for h in range(2):
        got(wz_buf.at[h, pl.ds(0, 7)], W_Z + h)
        for s in range(8):
            wz_wide[s] = wz_buf[h, s].astype(F32)
            for q in range(4):
                asm[12 * s:12 * s + 12, 128 * q:128 * q + 128] = wz_wide[s, 12 * q:12 * q + 12, :]
        wb[h, k, x] = asm[...].astype(BF16)
        own = piece(h, x)
        at = RING + 10 * h
        copy(own.at[low], own.at[low], at, right).start()
        copy(own.at[high], own.at[high], at + 2, left).start()
        copy(own.at[high], own.at[high], at + 1, right).start()
        copy(own.at[low], own.at[low], at + 3, left).start()
        copy(own, own, at + 6, core).start()
        if h == 0:
            got(fz_buf.at[pl.ds(0, 7)], F_Z)
            for buf, at in ((ft, 0), (fs, 24)):
                v = [fz_buf[d, :, :].astype(F32) for d in range(8)]
                v = [jnp.concatenate([m[at + 8 * n:at + 8 * n + 8] for m in v], axis=0) for n in range(3)]
                buf[y] = jnp.concatenate(v, axis=1).astype(BF16)
            rows_out(ft, T_Y)
        else:
            rows_on(ft, T_Y)
            rows_out(fs, S_Y)

    def relay(h):
        at, from_left, from_right = RING + 10 * h, piece(h, x_left), piece(h, x_right)
        got(from_left.at[low], at)
        copy(from_left.at[low], from_left.at[low], at + 4, right).start()
        got(from_right.at[high], at + 2)
        copy(from_right.at[high], from_right.at[high], at + 5, left).start()
        got(from_left.at[high], at + 1)
        copy(from_left, from_left, at + 7, core).start()
        got(from_right.at[low], at + 3)
        copy(from_right, from_right, at + 8, core).start()

    def far_piece(h):
        far = piece(h, x_far)
        got(far.at[low], RING + 10 * h + 4)
        got(far.at[high], RING + 10 * h + 5)
        copy(far, far, RING + 10 * h + 9, core).start()

    relay(0)
    far_piece(0)
    relay(1)
    rows_in(ft, T_Y)

    def chunk(q):
        h, kk, c0 = lax.div(q, 4), lax.rem(lax.div(q, 2), 2), pl.multiple_of(lax.rem(q, 2) * 256, 256)
        return wb[h, kk, :, :, pl.ds(c0, 256)].reshape(384, 256), pl.ds(pl.multiple_of(q * 256, 256), 256)

    def teacher_chunk(q, carry):
        w, at = chunk(q)
        wf = w.astype(F32)
        inv = lax.rsqrt(jnp.sum(wf * wf, axis=0, keepdims=True) + EPS)
        scores = jnp.dot(ft[...].reshape(512, 384), w, preferred_element_type=F32)
        e = jnp.exp2(scores * (inv * T_SCALE))
        e_ref[:, at] = e
        col = jnp.sum(e, axis=0, keepdims=True)
        for n in range(2):
            part = slice(128 * n, 128 * n + 128)
            ivec[pl.ds(2 * q + n, 1), :] = inv[:, part]
            csum[pl.ds(2 * q + n, 1), :] = col[:, part]
        return carry

    def teacher_part(h, kk):
        lax.fori_loop(0, 2, lambda c, carry: teacher_chunk(4 * h + 2 * kk + c, carry), 0)

    for h in range(2):
        if h == 1:
            far_piece(1)
        teacher_part(h, k)
        if h == 1:
            rows_on(fs, S_Y)
        for n in range(4):
            got(piece(h, x), RING + 10 * h + 6 + n)
        teacher_part(h, 1 - k)

    def columns_start(it):
        c_send[it] = csum[...].astype(BF16)
        for i in FAR_FIRST:
            copy(c_send.at[it], c_buf.at[it, i - 1], COLS + it, xk_peer(i)).start()

    def columns_end(it):
        got(c_buf.at[it], COLS + it)
        cvec[...] = 1.0 / fold([c_send[it].astype(F32)] + [c_buf[it, i].astype(F32) for i in range(7)])

    def row_pass():
        scale = [cvec[q:q + 1, :] for q in range(16)]

        def body(i, carry):
            rows = pl.ds(pl.multiple_of(i * 16, 16), 16)
            rowacc[rows, :] = fold([e_ref[rows, 128 * q:128 * q + 128] * scale[q] for q in range(16)])
            return carry

        lax.fori_loop(0, 32, body, 0, unroll=4)

    def lanes(ref):
        return [jnp.sum(jnp.transpose(ref[128 * j:128 * j + 128, :]), axis=0, keepdims=True) for j in range(4)]

    def put(dst, at, sums):
        for j in range(4):
            dst[at + j:at + j + 1, :] = sums[j]

    def tree(terms):
        while len(terms) > 1:
            pairs = [a + b for a, b in zip(terms[::2], terms[1::2])]
            terms = pairs + terms[2 * len(pairs):]
        return terms[0]

    def added(own, buf):
        return tree([own[...]] + [buf[i] for i in range(buf.shape[0])])

    def turn(row):
        return jnp.transpose(jnp.broadcast_to(row, (128, 128)))

    def set_row_scale(total):
        r = 1.0 / total[0:4, :]
        for j in range(4):
            rb[128 * j:128 * j + 128, :] = turn(r[j:j + 1, :])

    def rows_start(it):
        put(r_send.at[it], 0, lanes(rowacc))
        for n, (i, j) in enumerate(plane):
            copy(r_send.at[it], r_buf.at[it, n], ROWS + it, plane_peer(i, j)).start()

    def rows_end(it):
        got(r_buf.at[it], ROWS + it)
        set_row_scale(added(r_send.at[it], r_buf.at[it]))

    def last_rows_start():
        put(lry_send, 0, lanes(rowacc))
        for i in FAR_FIRST:
            copy(lry_send, lry_buf.at[i - 1], LAST_Y, y_peer(i)).start()

    def last_rows_middle():
        got(lry_buf, LAST_Y)
        lrz_send[...] = added(lry_send, lry_buf)
        for i in FAR_FIRST:
            copy(lrz_send, lrz_buf.at[i - 1], LAST_Z, z_peer(i)).start()

    def last_rows_end():
        got(lrz_buf, LAST_Z)
        total = added(lrz_send, lrz_buf)
        set_row_scale(total)
        return total

    def column_pass():
        def body(i, acc):
            rows = pl.ds(pl.multiple_of(i * 8, 8), 8)
            r8 = rb[rows, :]
            return tuple(acc[q] + e_ref[rows, 128 * q:128 * q + 128] * r8 for q in range(16))

        acc = lax.fori_loop(0, 64, body, tuple(jnp.zeros((8, 128), F32) for _ in range(16)), unroll=4)
        for q in range(16):
            csum[q:q + 1, :] = jnp.sum(acc[q], axis=0, keepdims=True)

    def student_chunk(q, carry):
        w, at = chunk(q)
        inv = jnp.concatenate([ivec[pl.ds(2 * q, 1), :], ivec[pl.ds(2 * q + 1, 1), :]], axis=1)
        logits = jnp.dot(fs[...].reshape(512, 384), w, preferred_element_type=F32) * (inv * S_SCALE)
        l_ref[:, at] = logits
        p = jnp.exp2(logits)
        eacc[...] += p[:, :128] + p[:, 128:]
        pb[:, at] = (p * inv).astype(BF16)
        return carry

    def product(first, last):
        total = None
        for n in range(4):
            h, kk = divmod(n, 2)
            term = lax.dot_general(
                pb[:, 512 * n:512 * n + 512], wb[h, kk].reshape(384, 512)[first:last], NT, preferred_element_type=F32
            )
            total = term if total is None else total + term
        return total

    def gradient(p, dst):
        gs[...] = product(128 * p, 128 * p + 128)
        for i in range(8):
            at = [crops(i, j) if p < 2 else crops(j, i) for j in range(8)]
            dst[p, i] = jnp.concatenate([gs[rows, :] for rows in at], axis=0).astype(BF16)

    def spread(p, src, dst, sem):
        me, peer = (a_me, a_peer) if p < 2 else (b_me, b_peer)
        for i in FAR_FIRST:
            copy(src.at[p, lax.rem(me + i, 8)], dst.at[p, i - 1], sem + p, peer(i)).start()

    def gathered(p, src, dst, sem):
        got(dst.at[p], sem + p)
        own = src[p, a_me if p < 2 else b_me]
        return fold([own.astype(F32)] + [dst[p, i].astype(F32) for i in range(7)])

    def students(first, last):
        lax.fori_loop(first, last, student_chunk, 0)

    columns_start(0)
    lry_send[...] = jnp.zeros_like(lry_send)
    eacc[...] = jnp.zeros_like(eacc)
    rows_in(fs, S_Y)
    students(0, 2)
    columns_end(0)
    row_pass()
    rows_start(0)
    students(2, 5)
    rows_end(0)
    column_pass()
    columns_start(1)
    students(5, 8)
    columns_end(1)
    row_pass()
    rows_start(1)
    gradient(0, g1_send)
    gradient(1, g1_send)
    rows_end(1)
    spread(0, g1_send, g1_buf, G1)
    column_pass()
    columns_start(2)
    spread(1, g1_send, g1_buf, G1)
    gradient(2, g1_send)
    spread(2, g1_send, g1_buf, G1)
    loads[3].wait()
    col_cot[...] = turn(cot_ref[...])
    s16 = unit_rows(s_ref[...].astype(F32))
    s8, inv8 = (jnp.where(half == 0, v[0:8], v[8:16]) for v in s16)
    put(lry_send, 8, lanes(eacc))
    own_unit[...] = jnp.dot(s8, perm_ref[...].astype(F32), precision=HIGHEST, preferred_element_type=F32)
    columns_end(2)

    c_rows = [cvec[q:q + 1, :] for q in range(16)]
    i_rows = [ivec[q:q + 1, :] for q in range(16)]

    def last_pass(i, carry):
        rows = pl.ds(pl.multiple_of(i * 16, 16), 16)
        acc, acc2 = [], []
        for q in range(16):
            at = slice(128 * q, 128 * q + 128)
            v = e_ref[rows, at] * c_rows[q]
            acc.append(v)
            acc2.append(v * l_ref[rows, at])
            pb[rows, at] = (v * i_rows[q]).astype(BF16)
        rowacc[rows, :] = fold(acc)
        rowacc2[rows, :] = fold(acc2)
        return carry

    lax.fori_loop(0, 32, last_pass, 0, unroll=2)
    put(lry_send, 4, lanes(rowacc2))
    last_rows_start()
    gradient(0, g2_send)
    spread(0, g2_send, g2_buf, G2)
    gradient(2, g2_send)
    spread(2, g2_send, g2_buf, G2)
    gradient(1, g2_send)
    spread(1, g2_send, g2_buf, G2)
    last_rows_middle()

    def wide(block, times):
        return jnp.concatenate([block] * times, axis=1)

    g1 = [gathered(p, g1_send, g1_buf, G1) for p in range(3)]
    total = last_rows_end()
    vec[...] = total
    inv_total = 1.0 / total[8:12, :]
    for j in range(4):
        xb[128 * j:128 * j + 128, :] = turn(inv_total[j:j + 1, :])
    col_x[...] = turn(vec[pl.ds(lax.div(y, 2) + 4, 1), :])
    g2b = gathered(2, g2_send, g2_buf, G2)
    for a in range(8):
        rows, part = crops(a, b_me), slice(8 * a, 8 * a + 8)
        ub_send[a] = g1[2][part] * xb[rows, :] - g2b[part] * rb[rows, :]
    for i in FAR_FIRST:
        copy(ub_send.at[lax.rem(a_me + i, 8)], ub_buf.at[i - 1], U_B, a_peer(i)).start()
    g2a = [gathered(p, g2_send, g2_buf, G2) for p in range(2)]
    for b in range(8):
        rows, part = crops(a_me, b), slice(8 * b, 8 * b + 8)
        u = [g1[p][part] * xb[rows, :] - g2a[p][part] * rb[rows, :] for p in range(2)]
        ua_send[b] = jnp.concatenate(u, axis=0)
    for i in FAR_FIRST:
        copy(ua_send.at[lax.rem(b_me + i, 8)], ua_buf.at[i - 1], U_A, b_peer(i)).start()

    rows8 = pl.ds(pl.multiple_of(y * 64 + z * 8, 8), 8)
    cross = rb[rows8, :] * col_x[pl.ds(pl.multiple_of(half * 64 + z * 8, 8), 8), :]
    loss8 = -jnp.log(xb[rows8, :]) - math.log(2.0) * cross
    cot8 = wide(col_cot[pl.ds(pl.multiple_of(k * 64 + y * 8, 8), 8), :], 3)
    got(ub_buf, U_B)
    u_b = added(ub_send.at[a_me], ub_buf)
    got(ua_buf, U_A)
    u_a = added(ua_send.at[b_me], ua_buf)
    u8 = jnp.concatenate([u_a[:8], u_a[8:], u_b], axis=1) * (cot8 / 0.1)
    unit8 = own_unit[...]
    along = jnp.sum(unit8 * u8, axis=1, keepdims=True)
    result = ((u8 - unit8 * along) * inv8).astype(BF16)
    result = lax.dot_general(result, perm_ref[...], NT, preferred_element_type=F32)
    first = loss8.astype(BF16).astype(F32)
    loss8 = jnp.where(lax.broadcasted_iota(jnp.int32, (8, 128), 1) < 64, first, loss8 - first)
    low_rows, high_rows = result[:, :256], jnp.concatenate([result[:, 256:], loss8], axis=1)
    result = jnp.concatenate([low_rows, high_rows], axis=0).astype(BF16)
    fin_send[...] = result
    slot = k * 8 + y
    fin_buf[slot] = result
    for i in FAR_FIRST:
        copy(fin_send, fin_buf.at[slot], FIN, y_peer(i)).start()
        copy(fin_send, fin_buf.at[slot], FIN, y_cross(i)).start()
    copy(fin_send, fin_buf.at[slot], FIN, core).start()
    got(fin_buf.at[pl.ds(0, 15)], FIN)
    out = fin_buf[...].astype(F32)
    grad_ref[:, :256] = out[:, :8, :].reshape(128, 256)
    grad_ref[:, 256:] = out[:, 8:, :128].reshape(128, 128)
    losses = jnp.transpose(out[:, 8:, 128:].reshape(128, 128))
    loss_ref[...] = losses[0:1, :] + losses[64:65, :]

    sent(fz_buf.at[pl.ds(0, 7)], F_Z)
    for buf, at in ((ft, T_Y), (fs, S_Y)):
        sent(buf.at[pl.ds(0, 2)], at)
        sent(buf.at[y], at + 1)
        sent(buf.at[y], at + 2)
        sent(buf.at[pl.ds(0, 3)], at + 3)
    for h in range(2):
        at, own = RING + 10 * h, piece(h, x)
        sent(wz_buf.at[h, pl.ds(0, 7)], W_Z + h)
        for n in range(6):
            sent(own.at[low], at + n)
        for n in range(6, 10):
            sent(own, at + n)
    for it in range(3):
        sent(c_buf.at[it], COLS + it)
    for it in range(2):
        sent(r_buf.at[it], ROWS + it)
    sent(lry_buf, LAST_Y)
    sent(lrz_buf, LAST_Z)
    for p in range(3):
        sent(g1_buf.at[p], G1 + p)
        sent(g2_buf.at[p], G2 + p)
    for buf, sem in (
        (ua_buf, U_A), (ub_buf, U_B),
        (fin_buf.at[pl.ds(0, 15)], FIN),
    ):
        sent(buf, sem)


def shards(teacher, student, proto_weight, cotangent):
    vmem, hbm = pl.BlockSpec(memory_space=pltpu.VMEM), pl.BlockSpec(memory_space=pltpu.HBM)
    v = pltpu.VMEM
    operands = (teacher, student, proto_weight, cotangent.reshape(1, 128))
    grad, loss = pl.pallas_call(
        kernel,
        out_shape=(v((128, 384), F32), v((1, 128), F32)),
        in_specs=[hbm] * 4,
        out_specs=(vmem, vmem),
        scratch_shapes=[
            v((16, 384), BF16), v((16, 384), BF16), v((12, 8192), BF16), v((1, 128), F32), v((384, 384), BF16),
            v((768, 128), F32), v((2, 8, 48, 128), BF16), v((2, 8, 48, 128), BF16), v((8, 48, 128), F32),
            v((96, 512), F32), v((2, 2, 4, 96, 512), BF16),
            v((48, 128), BF16), v((8, 48, 128), BF16), v((8, 64, 384), BF16), v((8, 64, 384), BF16),
            v((512, 2048), F32), v((512, 2048), F32), v((512, 2048), BF16),
            v((512, 128), F32), v((512, 128), F32), v((512, 128), F32), v((512, 128), F32), v((512, 128), F32),
            v((16, 128), F32), v((16, 128), F32),
            v((3, 16, 128), BF16), v((3, 7, 16, 128), BF16),
            v((2, 4, 128), F32), v((2, 63, 4, 128), F32),
            v((512, 128), F32),
            v((3, 8, 64, 128), BF16), v((3, 7, 64, 128), BF16), v((3, 8, 64, 128), BF16), v((3, 7, 64, 128), BF16),
            v((8, 16, 128), F32), v((7, 16, 128), F32), v((8, 8, 128), F32), v((7, 8, 128), F32),
            v((16, 128), F32), v((16, 128), F32), v((16, 128), F32), v((7, 16, 128), F32), v((16, 128), F32), v((7, 16, 128), F32),
            v((128, 128), F32), v((128, 128), F32), v((8, 384), F32),
            v((16, 256), BF16), v((16, 16, 256), BF16),
            pltpu.SemaphoreType.DMA((4,)), pltpu.SemaphoreType.DMA((COUNT,)), pltpu.SemaphoreType.DMA((COUNT,)),
        ],
        compiler_params=pltpu.CompilerParams(
            collective_id=0, has_side_effects=True, vmem_limit_bytes=60 * 1024 * 1024
        ),
        cost_estimate=pl.CostEstimate(flops=2_400_000_000, bytes_accessed=4_000_000, transcendentals=2_000_000),
    )(*(pltpu.with_memory_space_constraint(a, pltpu.HBM) for a in operands))
    return loss.reshape(128), grad


def solution(mesh):
    return jax.shard_map(
        shards,
        mesh=mesh,
        in_specs=(P("dp", None), P("dp", None), P("dp", "proto"), P("dp")),
        out_specs=(P("dp"), P("dp", None)),
        check_vma=False,
    )
```

```python
import math

import jax
import jax.numpy as jnp
from jax import lax
from jax.experimental import pallas as pl
from jax.experimental.pallas import tpu as pltpu
from jax.sharding import PartitionSpec as P

EPS = 1e-06
LOG2E = math.log2(math.e)
T_SCALE = LOG2E / 0.04
S_SCALE = LOG2E / 0.1
F32, BF16 = jnp.float32, jnp.bfloat16
MESH = pl.DeviceIdType.MESH
HIGHEST = lax.Precision.HIGHEST
NT = (((1,), (1,)), ((), ()))

FAR_FIRST = (4, 3, 5, 2, 6, 1, 7)

F_Z, W_Z = 0, 1
RING = 4
COLS = 24
ROWS, LAST_Y, LAST_Z = 27, 29, 30
G1, G2 = 33, 36
U_A, U_B, FIN = 39, 40, 41
T_Y, S_Y = 42, 46
EXP_Y, EXP_Z = 50, 51
COUNT = 52


def unit_rows(values):
    inv = lax.rsqrt(jnp.sum(values * values, axis=1, keepdims=True) + EPS)
    return values * inv, inv


def fold(terms):
    while len(terms) > 1:
        terms = [a + b for a, b in zip(terms[::2], terms[1::2])]
    return terms[0]


def kernel(
    t_hbm, s_hbm, w_hbm, cot_hbm,
    grad_ref, loss_ref,
    t_ref, s_ref, w_ref, cot_ref, perm_ref,
    pack, wz_send, wz_buf, wz_wide, asm, wb,
    fz_send, fz_buf, ft, fs,
    e_ref, l_ref, pb, rowacc, rowacc2, eacc, rb, xb, ivec, cvec,
    c_send, c_buf, r_send, r_buf,
    gs, g1_send, g1_buf, g2_send, g2_buf,
    ua_send, ua_buf, ub_send, ub_buf, csum, vec, lry_send, lry_buf, lrz_send, lrz_buf,
    ey_send, ey_buf, ez_send, ez_buf,
    col_cot, col_x, own_unit,
    fin_send, fin_buf,
    lsem, ssem, rsem,
):
    dp, pr = lax.axis_index("dp"), lax.axis_index("proto")
    z, x = lax.div(dp, 4), lax.rem(dp, 4)
    y, k = lax.div(pr, 2), lax.rem(pr, 2)

    def z_peer(i):
        return (lax.rem(z + i, 8) * 4 + x, pr)

    def y_peer(i):
        return (dp, lax.rem(y + i, 8) * 2 + k)

    def xk_peer(i):
        g = lax.rem(x * 2 + k + i, 8)
        return (z * 4 + lax.div(g, 2), y * 2 + lax.rem(g, 2))

    def plane_peer(i, j):
        return (z_peer(i)[0], y_peer(j)[1])

    plane = [(i, j) for i in FAR_FIRST + (0,) for j in FAR_FIRST + (0,)][:-1]

    def y_cross(i):
        return (dp, lax.rem(y + i, 8) * 2 + 1 - k)

    def a_peer(i):
        y_at, z_at = y_peer(i)[1], z_peer(i)[0]
        return (dp + k * (z_at - dp), y_at + k * (pr - y_at))

    def b_peer(i):
        y_at, z_at = y_peer(i)[1], z_peer(i)[0]
        return (z_at + k * (dp - z_at), pr + k * (y_at - pr))

    a_me, b_me = y + k * (z - y), z + k * (y - z)
    a_step, b_step = 64 - 56 * k, 8 + 56 * k

    def crops(a, b):
        return pl.ds(pl.multiple_of(a * a_step + b * b_step, 8), 8)

    def copy(src, dst, sem, peer):
        return pltpu.make_async_remote_copy(
            src_ref=src, dst_ref=dst, send_sem=ssem.at[sem], recv_sem=rsem.at[sem],
            device_id=peer, device_id_type=MESH,
        )

    def got(ref, sem):
        copy(ref, ref, sem, (dp, pr)).wait_recv()

    def sent(ref, sem):
        copy(ref, ref, sem, (dp, pr)).wait_send()

    half = lax.rem(y, 2)
    at16 = pl.multiple_of(k * 64 + lax.div(y, 2) * 16, 16)
    rows16 = pl.ds(at16, 16)
    loads = [
        pltpu.make_async_copy(src, dst, lsem.at[n])
        for n, (src, dst) in enumerate((
            (w_hbm, w_ref), (t_hbm.at[rows16], t_ref), (s_hbm.at[rows16], s_ref), (cot_hbm, cot_ref)
        ))
    ]
    for load in loads:
        load.start()

    barrier = pltpu.get_barrier_semaphore()
    for i in range(1, 8):
        for peer in (xk_peer(i), y_cross(i)):
            pl.semaphore_signal(barrier, inc=1, device_id=peer, device_id_type=MESH)
    for i, j in plane:
        pl.semaphore_signal(barrier, inc=1, device_id=plane_peer(i, j), device_id_type=MESH)

    feature = lax.broadcasted_iota(jnp.int32, (384, 128), 0)
    fz = lax.shift_right_logical(feature * 1366, 16)
    fx = lax.shift_right_logical((feature - fz * 48) * 5462, 16)
    place = fx * 96 + fz * 12 + (feature - fz * 48 - fx * 12)
    lane = lax.broadcasted_iota(jnp.int32, (384, 128), 1)
    for n in range(3):
        perm_ref[:, 128 * n:128 * n + 128] = (place == lane + 128 * n).astype(F32).astype(BF16)

    loads[0].wait()
    for d in range(8):
        for h in range(2):
            for r in range(4):
                q, at = d * 8 + h * 4 + r, ((h * 8 + d) * 4 + r) * 12
                pack[at:at + 12, :] = w_ref[:, 128 * q:128 * q + 128].astype(F32)
    for h in range(2):
        for d in range(8):
            at = (h * 8 + d) * 48
            wz_send[h, d] = pack[at:at + 48, :].astype(BF16)
        wz_buf[h, z] = wz_send[h, z]

    pl.semaphore_wait(barrier, 77)

    def weights_out(h):
        for i in FAR_FIRST:
            copy(wz_send.at[h, lax.rem(z + i, 8)], wz_buf.at[h, z], W_Z + h, z_peer(i)).start()

    weights_out(0)
    loads[1].wait()
    loads[2].wait()
    v = jnp.concatenate([t_ref[...].astype(F32), s_ref[...].astype(F32)], axis=0)
    v = jnp.dot(unit_rows(v)[0].astype(BF16), perm_ref[...], preferred_element_type=F32)
    v = [jnp.where(half == 0, v[at:at + 8], v[at + 8:at + 16]) for at in (0, 16)]
    v = jnp.concatenate([m[:, 128 * n:128 * n + 128] for m in v for n in range(3)], axis=0).astype(BF16)
    fz_send[...] = v
    fz_buf[z] = v
    for i in FAR_FIRST:
        copy(fz_send, fz_buf.at[z], F_Z, z_peer(i)).start()
    weights_out(1)

    first, second = pl.ds(0, 32), pl.ds(32, 32)

    def rows_out(buf, at):
        block = buf.at[y]
        copy(block, block, at + 1, y_peer(2)).start()
        copy(block, block, at + 2, y_peer(6)).start()
        copy(block, block, at, y_peer(1)).start()
        copy(block, block, at, y_peer(7)).start()

    def rows_on(buf, at):
        below, above = buf.at[lax.rem(y + 6, 8)], buf.at[lax.rem(y + 2, 8)]
        got(below, at + 1)
        copy(below.at[first], below.at[first], at + 3, y_peer(2)).start()
        copy(below, below, at + 3, y_peer(1)).start()
        got(above, at + 2)
        copy(above.at[second], above.at[second], at + 3, y_peer(6)).start()
        copy(above, above, at + 3, y_peer(7)).start()

    def rows_in(buf, at):
        got(buf.at[pl.ds(0, 2)], at)
        got(buf.at[pl.ds(0, 3)], at + 3)

    x_right, x_left, x_far = lax.rem(x + 1, 4), lax.rem(x + 3, 4), lax.rem(x + 2, 4)
    right, left, core = (z * 4 + x_right, pr), (z * 4 + x_left, pr), (dp, y * 2 + 1 - k)
    low, high = pl.ds(0, 48), pl.ds(48, 48)

    def piece(h, at):
        return wb.at[h, k, at]

    for h in range(2):
        got(wz_buf.at[h, pl.ds(0, 7)], W_Z + h)
        for s in range(8):
            wz_wide[s] = wz_buf[h, s].astype(F32)
            for q in range(4):
                asm[12 * s:12 * s + 12, 128 * q:128 * q + 128] = wz_wide[s, 12 * q:12 * q + 12, :]
        wb[h, k, x] = asm[...].astype(BF16)
        own = piece(h, x)
        at = RING + 10 * h
        copy(own.at[low], own.at[low], at, right).start()
        copy(own.at[high], own.at[high], at + 2, left).start()
        copy(own.at[high], own.at[high], at + 1, right).start()
        copy(own.at[low], own.at[low], at + 3, left).start()
        copy(own, own, at + 6, core).start()
        if h == 0:
            got(fz_buf.at[pl.ds(0, 7)], F_Z)
            for buf, at in ((ft, 0), (fs, 24)):
                v = [fz_buf[d, :, :].astype(F32) for d in range(8)]
                v = [jnp.concatenate([m[at + 8 * n:at + 8 * n + 8] for m in v], axis=0) for n in range(3)]
                buf[y] = jnp.concatenate(v, axis=1).astype(BF16)
            rows_out(ft, T_Y)
        else:
            rows_on(ft, T_Y)
            rows_out(fs, S_Y)

    def relay(h):
        at, from_left, from_right = RING + 10 * h, piece(h, x_left), piece(h, x_right)
        got(from_left.at[low], at)
        copy(from_left.at[low], from_left.at[low], at + 4, right).start()
        got(from_right.at[high], at + 2)
        copy(from_right.at[high], from_right.at[high], at + 5, left).start()
        got(from_left.at[high], at + 1)
        copy(from_left, from_left, at + 7, core).start()
        got(from_right.at[low], at + 3)
        copy(from_right, from_right, at + 8, core).start()

    def far_piece(h):
        far = piece(h, x_far)
        got(far.at[low], RING + 10 * h + 4)
        got(far.at[high], RING + 10 * h + 5)
        copy(far, far, RING + 10 * h + 9, core).start()

    relay(0)
    far_piece(0)
    relay(1)
    rows_in(ft, T_Y)

    def chunk(q):
        h, kk, c0 = lax.div(q, 4), lax.rem(lax.div(q, 2), 2), pl.multiple_of(lax.rem(q, 2) * 256, 256)
        return wb[h, kk, :, :, pl.ds(c0, 256)].reshape(384, 256), pl.ds(pl.multiple_of(q * 256, 256), 256)

    def teacher_chunk(q, carry):
        w, at = chunk(q)
        wf = w.astype(F32)
        inv = lax.rsqrt(jnp.sum(wf * wf, axis=0, keepdims=True) + EPS)
        scores = jnp.dot(ft[...].reshape(512, 384), w, preferred_element_type=F32)
        e = jnp.exp2(scores * (inv * T_SCALE))
        e_ref[:, at] = e
        col = jnp.sum(e, axis=0, keepdims=True)
        for n in range(2):
            part = slice(128 * n, 128 * n + 128)
            ivec[pl.ds(2 * q + n, 1), :] = inv[:, part]
            csum[pl.ds(2 * q + n, 1), :] = col[:, part]
        return carry

    def teacher_part(h, kk):
        lax.fori_loop(0, 2, lambda c, carry: teacher_chunk(4 * h + 2 * kk + c, carry), 0)

    for h in range(2):
        if h == 1:
            far_piece(1)
        teacher_part(h, k)
        if h == 1:
            rows_on(fs, S_Y)
        for n in range(4):
            got(piece(h, x), RING + 10 * h + 6 + n)
        teacher_part(h, 1 - k)

    def columns_start(it):
        c_send[it] = csum[...].astype(BF16)
        for i in FAR_FIRST:
            copy(c_send.at[it], c_buf.at[it, i - 1], COLS + it, xk_peer(i)).start()

    def columns_end(it):
        got(c_buf.at[it], COLS + it)
        cvec[...] = 1.0 / fold([c_send[it].astype(F32)] + [c_buf[it, i].astype(F32) for i in range(7)])

    def row_pass():
        scale = [cvec[q:q + 1, :] for q in range(16)]

        def body(i, carry):
            rows = pl.ds(pl.multiple_of(i * 16, 16), 16)
            rowacc[rows, :] = fold([e_ref[rows, 128 * q:128 * q + 128] * scale[q] for q in range(16)])
            return carry

        lax.fori_loop(0, 32, body, 0, unroll=4)

    def lanes(ref):
        return [jnp.sum(jnp.transpose(ref[128 * j:128 * j + 128, :]), axis=0, keepdims=True) for j in range(4)]

    def put(dst, at, sums):
        for j in range(4):
            dst[at + j:at + j + 1, :] = sums[j]

    def tree(terms):
        while len(terms) > 1:
            pairs = [a + b for a, b in zip(terms[::2], terms[1::2])]
            terms = pairs + terms[2 * len(pairs):]
        return terms[0]

    def added(own, buf):
        return tree([own[...]] + [buf[i] for i in range(buf.shape[0])])

    def turn(row):
        return jnp.transpose(jnp.broadcast_to(row, (128, 128)))

    def set_row_scale(total):
        r = 1.0 / total[0:4, :]
        for j in range(4):
            rb[128 * j:128 * j + 128, :] = turn(r[j:j + 1, :])

    def rows_start(it):
        put(r_send.at[it], 0, lanes(rowacc))
        for n, (i, j) in enumerate(plane):
            copy(r_send.at[it], r_buf.at[it, n], ROWS + it, plane_peer(i, j)).start()

    def rows_end(it):
        got(r_buf.at[it], ROWS + it)
        set_row_scale(added(r_send.at[it], r_buf.at[it]))

    def last_rows_start():
        put(lry_send, 0, lanes(rowacc))
        for i in FAR_FIRST:
            copy(lry_send, lry_buf.at[i - 1], LAST_Y, y_peer(i)).start()

    def last_rows_middle():
        got(lry_buf, LAST_Y)
        lrz_send[...] = added(lry_send, lry_buf)
        for i in FAR_FIRST:
            copy(lrz_send, lrz_buf.at[i - 1], LAST_Z, z_peer(i)).start()

    def last_rows_end():
        got(lrz_buf, LAST_Z)
        total = added(lrz_send, lrz_buf)
        set_row_scale(total)
        return total

    def column_pass():
        def body(i, acc):
            rows = pl.ds(pl.multiple_of(i * 8, 8), 8)
            r8 = rb[rows, :]
            return tuple(acc[q] + e_ref[rows, 128 * q:128 * q + 128] * r8 for q in range(16))

        acc = lax.fori_loop(0, 64, body, tuple(jnp.zeros((8, 128), F32) for _ in range(16)), unroll=4)
        for q in range(16):
            csum[q:q + 1, :] = jnp.sum(acc[q], axis=0, keepdims=True)

    def student_chunk(q, carry):
        w, at = chunk(q)
        inv = jnp.concatenate([ivec[pl.ds(2 * q, 1), :], ivec[pl.ds(2 * q + 1, 1), :]], axis=1)
        logits = jnp.dot(fs[...].reshape(512, 384), w, preferred_element_type=F32) * (inv * S_SCALE)
        l_ref[:, at] = logits
        p = jnp.exp2(logits)
        eacc[...] += p[:, :128] + p[:, 128:]
        pb[:, at] = (p * inv).astype(BF16)
        return carry

    def product(first, last):
        total = None
        for n in range(4):
            h, kk = divmod(n, 2)
            term = lax.dot_general(
                pb[:, 512 * n:512 * n + 512], wb[h, kk].reshape(384, 512)[first:last], NT, preferred_element_type=F32
            )
            total = term if total is None else total + term
        return total

    def gradient(p, dst):
        gs[...] = product(128 * p, 128 * p + 128)
        for i in range(8):
            at = [crops(i, j) if p < 2 else crops(j, i) for j in range(8)]
            dst[p, i] = jnp.concatenate([gs[rows, :] for rows in at], axis=0).astype(BF16)

    def spread(p, src, dst, sem):
        me, peer = (a_me, a_peer) if p < 2 else (b_me, b_peer)
        for i in FAR_FIRST:
            copy(src.at[p, lax.rem(me + i, 8)], dst.at[p, i - 1], sem + p, peer(i)).start()

    def gathered(p, src, dst, sem):
        got(dst.at[p], sem + p)
        own = src[p, a_me if p < 2 else b_me]
        return fold([own.astype(F32)] + [dst[p, i].astype(F32) for i in range(7)])

    def students(first, last):
        lax.fori_loop(first, last, student_chunk, 0)

    columns_start(0)
    eacc[...] = jnp.zeros_like(eacc)
    rows_in(fs, S_Y)
    students(0, 2)
    columns_end(0)
    row_pass()
    rows_start(0)
    students(2, 5)
    rows_end(0)
    column_pass()
    columns_start(1)
    students(5, 8)
    put(ey_send, 0, lanes(eacc))
    for i in FAR_FIRST:
        copy(ey_send, ey_buf.at[i - 1], EXP_Y, y_peer(i)).start()
    columns_end(1)
    row_pass()
    rows_start(1)
    gradient(0, g1_send)
    gradient(1, g1_send)
    got(ey_buf, EXP_Y)
    ez_send[...] = added(ey_send, ey_buf)
    for i in FAR_FIRST:
        copy(ez_send, ez_buf.at[i - 1], EXP_Z, z_peer(i)).start()
    rows_end(1)
    spread(0, g1_send, g1_buf, G1)
    column_pass()
    columns_start(2)
    spread(1, g1_send, g1_buf, G1)
    gradient(2, g1_send)
    spread(2, g1_send, g1_buf, G1)
    loads[3].wait()
    col_cot[...] = turn(cot_ref[...])
    s16 = unit_rows(s_ref[...].astype(F32))
    s8, inv8 = (jnp.where(half == 0, v[0:8], v[8:16]) for v in s16)
    got(ez_buf, EXP_Z)
    inv_total = 1.0 / added(ez_send, ez_buf)
    for j in range(4):
        xb[128 * j:128 * j + 128, :] = turn(inv_total[j:j + 1, :])
    own_unit[...] = jnp.dot(s8, perm_ref[...].astype(F32), precision=HIGHEST, preferred_element_type=F32)
    columns_end(2)

    c_rows = [cvec[q:q + 1, :] for q in range(16)]
    i_rows = [ivec[q:q + 1, :] for q in range(16)]

    def last_pass(i, carry):
        rows = pl.ds(pl.multiple_of(i * 16, 16), 16)
        acc, acc2 = [], []
        for q in range(16):
            at = slice(128 * q, 128 * q + 128)
            v = e_ref[rows, at] * c_rows[q]
            acc.append(v)
            acc2.append(v * l_ref[rows, at])
            pb[rows, at] = (v * i_rows[q]).astype(BF16)
        rowacc[rows, :] = fold(acc)
        rowacc2[rows, :] = fold(acc2)
        return carry

    lax.fori_loop(0, 32, last_pass, 0, unroll=2)
    put(lry_send, 4, lanes(rowacc2))
    last_rows_start()
    gradient(0, g2_send)
    spread(0, g2_send, g2_buf, G2)
    gradient(2, g2_send)
    spread(2, g2_send, g2_buf, G2)
    gradient(1, g2_send)
    spread(1, g2_send, g2_buf, G2)
    last_rows_middle()

    def wide(block, times):
        return jnp.concatenate([block] * times, axis=1)

    g1 = [gathered(p, g1_send, g1_buf, G1) for p in range(3)]
    total = last_rows_end()
    vec[...] = total
    col_x[...] = turn(vec[pl.ds(lax.div(y, 2) + 4, 1), :])
    g2b = gathered(2, g2_send, g2_buf, G2)
    for a in range(8):
        rows, part = crops(a, b_me), slice(8 * a, 8 * a + 8)
        ub_send[a] = g1[2][part] * xb[rows, :] - g2b[part] * rb[rows, :]
    for i in FAR_FIRST:
        copy(ub_send.at[lax.rem(a_me + i, 8)], ub_buf.at[i - 1], U_B, a_peer(i)).start()
    g2a = [gathered(p, g2_send, g2_buf, G2) for p in range(2)]
    for b in range(8):
        rows, part = crops(a_me, b), slice(8 * b, 8 * b + 8)
        u = [g1[p][part] * xb[rows, :] - g2a[p][part] * rb[rows, :] for p in range(2)]
        ua_send[b] = jnp.concatenate(u, axis=0)
    for i in FAR_FIRST:
        copy(ua_send.at[lax.rem(b_me + i, 8)], ua_buf.at[i - 1], U_A, b_peer(i)).start()

    rows8 = pl.ds(pl.multiple_of(y * 64 + z * 8, 8), 8)
    cross = rb[rows8, :] * col_x[pl.ds(pl.multiple_of(half * 64 + z * 8, 8), 8), :]
    loss8 = -jnp.log(xb[rows8, :]) - math.log(2.0) * cross
    cot8 = wide(col_cot[pl.ds(pl.multiple_of(k * 64 + y * 8, 8), 8), :], 3)
    got(ub_buf, U_B)
    u_b = added(ub_send.at[a_me], ub_buf)
    got(ua_buf, U_A)
    u_a = added(ua_send.at[b_me], ua_buf)
    u8 = jnp.concatenate([u_a[:8], u_a[8:], u_b], axis=1) * (cot8 / 0.1)
    unit8 = own_unit[...]
    along = jnp.sum(unit8 * u8, axis=1, keepdims=True)
    result = ((u8 - unit8 * along) * inv8).astype(BF16)
    result = lax.dot_general(result, perm_ref[...], NT, preferred_element_type=F32)
    first = loss8.astype(BF16).astype(F32)
    loss8 = jnp.where(lax.broadcasted_iota(jnp.int32, (8, 128), 1) < 64, first, loss8 - first)
    low_rows, high_rows = result[:, :256], jnp.concatenate([result[:, 256:], loss8], axis=1)
    result = jnp.concatenate([low_rows, high_rows], axis=0).astype(BF16)
    fin_send[...] = result
    slot = k * 8 + y
    fin_buf[slot] = result
    for i in FAR_FIRST:
        copy(fin_send, fin_buf.at[slot], FIN, y_peer(i)).start()
        copy(fin_send, fin_buf.at[slot], FIN, y_cross(i)).start()
    copy(fin_send, fin_buf.at[slot], FIN, core).start()
    got(fin_buf.at[pl.ds(0, 15)], FIN)
    out = fin_buf[...].astype(F32)
    grad_ref[:, :256] = out[:, :8, :].reshape(128, 256)
    grad_ref[:, 256:] = out[:, 8:, :128].reshape(128, 128)
    losses = jnp.transpose(out[:, 8:, 128:].reshape(128, 128))
    loss_ref[...] = losses[0:1, :] + losses[64:65, :]

    sent(fz_buf.at[pl.ds(0, 7)], F_Z)
    for buf, at in ((ft, T_Y), (fs, S_Y)):
        sent(buf.at[pl.ds(0, 2)], at)
        sent(buf.at[y], at + 1)
        sent(buf.at[y], at + 2)
        sent(buf.at[pl.ds(0, 3)], at + 3)
    for h in range(2):
        at, own = RING + 10 * h, piece(h, x)
        sent(wz_buf.at[h, pl.ds(0, 7)], W_Z + h)
        for n in range(6):
            sent(own.at[low], at + n)
        for n in range(6, 10):
            sent(own, at + n)
    for it in range(3):
        sent(c_buf.at[it], COLS + it)
    for it in range(2):
        sent(r_buf.at[it], ROWS + it)
    sent(ey_buf, EXP_Y)
    sent(ez_buf, EXP_Z)
    sent(lry_buf, LAST_Y)
    sent(lrz_buf, LAST_Z)
    for p in range(3):
        sent(g1_buf.at[p], G1 + p)
        sent(g2_buf.at[p], G2 + p)
    for buf, sem in (
        (ua_buf, U_A), (ub_buf, U_B),
        (fin_buf.at[pl.ds(0, 15)], FIN),
    ):
        sent(buf, sem)


def shards(teacher, student, proto_weight, cotangent):
    vmem, hbm = pl.BlockSpec(memory_space=pltpu.VMEM), pl.BlockSpec(memory_space=pltpu.HBM)
    v = pltpu.VMEM
    operands = (teacher, student, proto_weight, cotangent.reshape(1, 128))
    grad, loss = pl.pallas_call(
        kernel,
        out_shape=(v((128, 384), F32), v((1, 128), F32)),
        in_specs=[hbm] * 4,
        out_specs=(vmem, vmem),
        scratch_shapes=[
            v((16, 384), BF16), v((16, 384), BF16), v((12, 8192), BF16), v((1, 128), F32), v((384, 384), BF16),
            v((768, 128), F32), v((2, 8, 48, 128), BF16), v((2, 8, 48, 128), BF16), v((8, 48, 128), F32),
            v((96, 512), F32), v((2, 2, 4, 96, 512), BF16),
            v((48, 128), BF16), v((8, 48, 128), BF16), v((8, 64, 384), BF16), v((8, 64, 384), BF16),
            v((512, 2048), F32), v((512, 2048), F32), v((512, 2048), BF16),
            v((512, 128), F32), v((512, 128), F32), v((512, 128), F32), v((512, 128), F32), v((512, 128), F32),
            v((16, 128), F32), v((16, 128), F32),
            v((3, 16, 128), BF16), v((3, 7, 16, 128), BF16),
            v((2, 4, 128), F32), v((2, 63, 4, 128), F32),
            v((512, 128), F32),
            v((3, 8, 64, 128), BF16), v((3, 7, 64, 128), BF16), v((3, 8, 64, 128), BF16), v((3, 7, 64, 128), BF16),
            v((8, 16, 128), F32), v((7, 16, 128), F32), v((8, 8, 128), F32), v((7, 8, 128), F32),
            v((16, 128), F32), v((8, 128), F32), v((8, 128), F32), v((7, 8, 128), F32), v((8, 128), F32), v((7, 8, 128), F32),
            v((4, 128), F32), v((7, 4, 128), F32), v((4, 128), F32), v((7, 4, 128), F32),
            v((128, 128), F32), v((128, 128), F32), v((8, 384), F32),
            v((16, 256), BF16), v((16, 16, 256), BF16),
            pltpu.SemaphoreType.DMA((4,)), pltpu.SemaphoreType.DMA((COUNT,)), pltpu.SemaphoreType.DMA((COUNT,)),
        ],
        compiler_params=pltpu.CompilerParams(
            collective_id=0, has_side_effects=True, vmem_limit_bytes=60 * 1024 * 1024
        ),
        cost_estimate=pl.CostEstimate(flops=2_400_000_000, bytes_accessed=4_000_000, transcendentals=2_000_000),
    )(*(pltpu.with_memory_space_constraint(a, pltpu.HBM) for a in operands))
    return loss.reshape(128), grad


def solution(mesh):
    return jax.shard_map(
        shards,
        mesh=mesh,
        in_specs=(P("dp", None), P("dp", None), P("dp", "proto"), P("dp")),
        out_specs=(P("dp"), P("dp", None)),
        check_vma=False,
    )
```
